256 devices in a mesh: group: 4 (over x_lo, core), dp: 8 (over z), tensor: 8 (over x_hi, y).
Axes of the slice: x: 4 (x_hi: 2, x_lo: 2; x = x_hi * 2 + x_lo), y: 4, z: 8, core: 2. Of those that a mesh axis runs over, the one named last changes fastest.
Arguments:
- images: float32 [8, 1024, 588], P('dp', 'tensor'), may hold values from 0 to 1
- step_size: float32 [8], P('dp'), may hold values from 0.05 to 0.25
- member_mask: int32 [4, 8], P('group', 'dp'), may hold values 0 or 1
- patch_weight: bfloat16 [4, 588, 1280], P('group'), may hold values from -0.25 to 0.25
- vision_norm_gain: float32 [4, 1280], P('group'), may hold values from 0.5 to 1.5
- merger_weight: bfloat16 [4, 5120, 8192], P('group', 'dp', 'tensor')
- norm_gain: float32 [4, 8192], P('group'), may hold values from 0.5 to 1.5
- kv_weight: bfloat16 [4, 2, 8192, 1024], P('group', None, 'dp', 'tensor'), may hold values from -0.0625 to 0.0625
- queries: bfloat16 [4, 8, 32, 8192], P('group', 'dp', None, 'tensor'), may hold values from -6 to 6
- cotangent: bfloat16 [4, 8, 32, 8192], P('group', 'dp', None, 'tensor'), may hold values from -6 to 6
Outputs:
- adversarial: float32 [8, 1024, 588], P('dp', 'tensor')
- direction: float32 [8, 1024, 588], P('dp', 'tensor')
The draws below stay inside these ranges and needn't reach their ends.
All inputs are finite; a program needn't handle non-finite values. No bound on the sum of `member_mask` on one device may be relied on, other than what follows from the above.
Results may differ from the reference program's by a relative error of at most 0.025.
Values may be sent and summed in bfloat16 or wider, within the bound.
A program may use at most 128 MiB of HBM per device.

```python
import math
import jax
import jax.numpy as jnp
from jax import lax

P_SIZE = 588
V = 1280
D = 8192
H = 64
KVH = 8
HD = 128
NP = 1024
CAP = 32
IMAGES = 8
MEMBERS = 4
N_GROUP = 4


def draw_images(key, part):
    key = jax.random.fold_in(key, 11)
    uniform_values = jax.random.uniform(key, (IMAGES, NP, P_SIZE), jnp.float32)
    position = jnp.arange(NP, dtype=jnp.float32) / (NP - 1)
    contrast = jnp.power(0.15, position)[None, :, None]
    return (uniform_values * contrast).astype(jnp.float32)


def draw_merger_weight(key, part):
    key = jax.random.fold_in(key, 23)
    entry_key, column_key = jax.random.split(key)
    entries = jnp.clip(jax.random.normal(entry_key, (MEMBERS, 4 * V, D), jnp.float32), -6.0, 6.0)
    position = jnp.arange(D, dtype=jnp.float32) / (D - 1)
    rise = jnp.power(6.0, position)
    jitter = jnp.exp(jax.random.uniform(column_key, (MEMBERS, 1, D), jnp.float32, jnp.log(0.7), jnp.log(1.4)))
    weights = entries * (4 * V) ** (-0.5) * rise[None, None, :] * jitter
    return weights.astype(jnp.bfloat16)


def with_ends(values, own_key, smallest, high):
    shape = values.shape
    index_at = [jax.random.randint(jax.random.fold_in(own_key, axis), (), 0, shape[axis]) for axis in range(len(shape))]
    values = values.at[tuple(index_at)].set(smallest)
    longest = shape.index(max(shape))
    index_at[longest] = (index_at[longest] + 1) % shape[longest]
    return values.at[tuple(index_at)].set(high)


def shard_levels(own_key, shape, cuts, smallest, largest):
    level, own = 1.0, jax.random.fold_in(own_key, 6)
    for dim, blocks in cuts:
        draws = jnp.exp(jax.random.uniform(jax.random.fold_in(own, dim), (blocks,), jnp.float32, smallest / len(cuts), largest / len(cuts)))
        level = level * jnp.repeat(draws, shape[dim] // blocks).reshape([-1 if axis == dim else 1 for axis in range(len(shape))])
    return level


def gaussian(rng, shape, deviation, bound, cuts=(), held_as=jnp.bfloat16):
    result = jax.random.normal(rng, shape, jnp.float32) * deviation
    if len(cuts) > 0:
        result = shard_levels(rng, shape, cuts, -0.22, 0.18) * result
    return jnp.clip(result, min=-bound, max=bound).astype(held_as)


def setup_inputs(seed: int = 0) -> dict:
    streams_of = jax.random.split(jax.random.key(seed), 11)
    images = draw_images(jax.random.fold_in(streams_of[10], 71), 0)
    step_size = jnp.clip(jnp.exp(math.log(0.25) - 1.609438 * jax.random.uniform(streams_of[1], (IMAGES,), jnp.float32) ** shard_levels(streams_of[1], (IMAGES,), ((0, 8),), -0.2, 0.2)), 0.05, 0.25)
    member_mask = with_ends((jax.random.randint(streams_of[2], (MEMBERS, IMAGES), 0, 4) < 3).astype(jnp.int32), jax.random.fold_in(streams_of[2], 1), 0, 1)
    patch_weight = gaussian(streams_of[3], (MEMBERS, P_SIZE, V), P_SIZE ** -0.5, 0.25, ((0, 4),))
    vision_norm_gain = jnp.clip(1.0 + 0.1 * jax.random.normal(streams_of[4], (MEMBERS, V), jnp.float32), 0.5, 1.5)
    merger_weight = draw_merger_weight(jax.random.fold_in(streams_of[10], 71), 0)
    norm_gain = jnp.clip(1.0 + 0.1 * jax.random.normal(streams_of[6], (MEMBERS, D), jnp.float32), 0.5, 1.5)
    kv_weight = gaussian(streams_of[7], (MEMBERS, 2, D, KVH * HD), D ** -0.5, 0.0625, ((0, 4), (2, 8), (3, 8)))
    queries = gaussian(streams_of[8], (MEMBERS, IMAGES, CAP, H * HD), 1.0, 6.0, ((0, 4), (1, 8), (3, 8)))
    cotangent = gaussian(streams_of[9], (MEMBERS, IMAGES, CAP, H * HD), 1.0, 6.0, ((0, 4), (1, 8), (3, 8)))
    return dict(images=images, step_size=step_size, member_mask=member_mask, patch_weight=patch_weight, vision_norm_gain=vision_norm_gain, merger_weight=merger_weight, norm_gain=norm_gain, kv_weight=kv_weight, queries=queries, cotangent=cotangent)


def rounded_values(value):
    return lax.optimization_barrier(value.astype(jnp.bfloat16)).astype(jnp.float32)

def reference(images, step_size, member_mask, patch_weight, vision_norm_gain, merger_weight, norm_gain, kv_weight, queries, cotangent):
    count = images.shape[0]
    tokens = NP // 4
    group_heads = H // KVH
    scale = 1.0 / math.sqrt(HD)
    pixels = rounded_values(images)
    gradient = jnp.zeros(images.shape, jnp.float32)
    for member_model in range(N_GROUP):
        patch_w = patch_weight[member_model].astype(jnp.float32)
        embed = jnp.einsum('inp,pv->inv', pixels, patch_w)
        centered_rows = embed - lax.optimization_barrier(jnp.mean(embed, -1, keepdims=True))
        inverse_deviation = lax.rsqrt(lax.optimization_barrier(jnp.mean(centered_rows * centered_rows, -1, keepdims=True)) + 1e-06)
        normalized_input = centered_rows * inverse_deviation
        visual_features = rounded_values(normalized_input * vision_norm_gain[member_model])
        merged = visual_features.reshape(count, tokens, 4 * V)
        merger_w = merger_weight[member_model].astype(jnp.float32)
        hidden = rounded_values(jnp.einsum('itr,rc->itc', merged, merger_w))
        gain = norm_gain[member_model]
        root = lax.rsqrt(lax.optimization_barrier(jnp.mean(hidden * hidden, -1, keepdims=True)) + 1e-06)
        features = rounded_values(hidden * root * gain)
        kv_full = kv_weight[member_model].astype(jnp.float32)
        keys_bf = rounded_values(jnp.einsum('itr,rc->itc', features, kv_full[0]))
        values_bf = rounded_values(jnp.einsum('itr,rc->itc', features, kv_full[1]))
        query = queries[member_model].astype(jnp.float32).reshape(count, CAP, KVH, group_heads, HD)
        key_heads = keys_bf.reshape(count, tokens, KVH, HD)
        value_heads = values_bf.reshape(count, tokens, KVH, HD)
        scores = jnp.einsum('icagd,itad->iagct', query, key_heads) * scale
        probs = jax.nn.softmax(scores, axis=-1)
        probs_bf = rounded_values(probs)
        weight_mask = member_mask[member_model].astype(jnp.float32)[:, None, None]
        grad_out = (cotangent[member_model].astype(jnp.float32) * weight_mask).reshape(query.shape)
        grad_probs = jnp.einsum('icagd,itad->iagct', grad_out, value_heads)
        inner = lax.optimization_barrier(jnp.sum(probs * grad_probs, -1, keepdims=True))
        grad_scores = rounded_values(probs * (grad_probs - inner) * scale)
        grad_values = rounded_values(jnp.einsum('iagct,icagd->itad', probs_bf, grad_out)).reshape(count, tokens, KVH * HD)
        grad_keys = rounded_values(jnp.einsum('iagct,icagd->itad', grad_scores, query)).reshape(count, tokens, KVH * HD)
        grad_feat = jnp.einsum('itc,rc->itr', grad_keys, kv_full[0]) + jnp.einsum('itc,rc->itr', grad_values, kv_full[1])
        row_sum = lax.optimization_barrier(jnp.sum(grad_feat * gain * hidden, -1, keepdims=True))
        grad_hidden = rounded_values(root * gain * grad_feat - hidden * root ** 3 * row_sum / D)
        grad_merged = jnp.einsum('itc,rc->itr', grad_hidden, merger_w)
        grad_visual = grad_merged.reshape(count, NP, V)
        gain_gradient = grad_visual * vision_norm_gain[member_model]
        embedding_gradient = rounded_values(inverse_deviation * (gain_gradient - lax.optimization_barrier(jnp.mean(gain_gradient, -1, keepdims=True)) - normalized_input * lax.optimization_barrier(jnp.mean(gain_gradient * normalized_input, -1, keepdims=True))))
        gradient = gradient + jnp.einsum('inv,pv->inp', embedding_gradient, patch_w)
    squares = lax.optimization_barrier(jnp.mean(gradient * gradient, axis=(1, 2), keepdims=True))
    direction = jnp.tanh(gradient * lax.rsqrt(squares + 1e-06))
    adversarial = jnp.clip(images + step_size[:, None, None] * direction, 0.0, 1.0)
    return (adversarial, direction)
```

```python
import functools
import math

import jax
import jax.numpy as jnp
from jax import lax
from jax.experimental import pallas as pl
from jax.experimental.pallas import tpu as pltpu
from jax.sharding import PartitionSpec as P

F32 = jnp.float32
BF16 = jnp.bfloat16
NZ = 8
NT = 8
NY = 4
L = 128
MESH = pl.DeviceIdType.MESH


def dot(a, b):
    return jnp.dot(a, b, preferred_element_type=F32)


def dot_nt(a, b):
    return lax.dot_general(a, b, (((1,), (1,)), ((), ())), preferred_element_type=F32)


def kernel(
    ng,
    n_pixels,
    pix,
    patch_w,
    vgain,
    w_ref,
    gain_ref,
    kv_ref,
    q_ref,
    cot_ref,
    mask_ref,
    out_ref,
    wg,
    kvl,
    tok,
    hid,
    part1,
    s1,
    r1,
    ssq_s,
    ssq_r,
    kvpre,
    kvt,
    kvh,
    gkvh,
    gkv,
    scal,
    part4,
    s4,
    r4,
    xhat,
    gbuf,
    sqb,
    local_sem,
    zs,
    zr,
    xs,
    xr,
    as_,
    ar,
    rs1s,
    rs1r,
    sqs,
    sqr,
    ats,
    atr,
    bts,
    btr,
    ags,
    agr,
    scs,
    scr,
    rs4s,
    rs4r,
    grs,
    grr,
    fs,
    fr,
):
    g = lax.axis_index("group")
    d = lax.axis_index("dp")
    t = lax.axis_index("tensor")
    x, y = t // NY, lax.rem(t, NY)
    rows = w_ref.shape[0]
    half_rows = (rows + 2 * L) // 2
    slot = tok.shape[2]
    ntok = NZ * slot

    def zmod(i):
        return lax.rem(i + 2 * NZ, NZ)

    def cols(i):
        return pl.ds(pl.multiple_of(i * L, L), L)

    def remote(src, dst, send, recv, **to):
        return pltpu.make_async_remote_copy(
            src_ref=src, dst_ref=dst, send_sem=send, recv_sem=recv, device_id=to, device_id_type=MESH
        )

    sent = []

    def start(copy):
        copy.start()
        sent.append(copy)

    barrier = pltpu.get_barrier_semaphore()
    for r in range(1, NZ):
        pl.semaphore_signal(barrier, inc=1, device_id={"dp": zmod(d + r)}, device_id_type=MESH)
    for r in range(1, NT):
        pl.semaphore_signal(barrier, inc=1, device_id={"tensor": lax.rem(t + r, NT)}, device_id_type=MESH)
    for r in range(1, ng):
        pl.semaphore_signal(barrier, inc=1, device_id={"group": lax.rem(g + r, ng)}, device_id_type=MESH)

    own = [
        pltpu.make_async_copy(w_ref.at[:, cols(d)], wg.at[d, pl.ds(0, rows), cols(t)], local_sem.at[0])
    ]
    for k in range(2):
        own.append(
            pltpu.make_async_copy(
                kv_ref.at[k, cols(d), :], wg.at[d, pl.ds(rows + L * k, L), cols(t)], local_sem.at[1 + k]
            )
        )
    for c in own:
        c.start()
    pl.semaphore_wait(barrier, NZ - 1 + NT - 1 + ng - 1)

    def offset(p):
        return (p + 1) // 2 * (1 if p % 2 else -1)

    for c in own:
        c.wait()

    up = x * NY + lax.rem(y + 1, NY)
    down = x * NY + lax.rem(y + NY - 1, NY)
    far = x * NY + lax.rem(y + 2, NY)
    xo = (1 - x) * NY
    across = xo + y
    whole, lo, hi = (0, 2 * half_rows), (0, half_rows), (half_rows, half_rows)
    kinds = (
        (t, up, down, whole),
        (t, down, up, whole),
        (t, across, across, whole),
        (down, up, far, lo),
        (up, down, far, hi),
        (across, up, xo + lax.rem(y + NY - 1, NY), whole),
        (across, down, xo + lax.rem(y + 1, NY), whole),
        (far, across, xo + lax.rem(y + 2, NY), whole),
    )

    def plane(p):
        step = (p + 1) // 2
        return zmod(d + jnp.where(lax.rem(p, 2) == 1, step, -step))

    def xy(kind, p, incoming=False):
        block, to, arrives, (at, size) = kinds[kind]
        view = wg.at[plane(p), pl.ds(at, size), cols(arrives if incoming else block)]
        return remote(view, view, xs.at[kind, p], xr.at[kind, p], tensor=to)

    def z_in(p, which):
        at, size = ((0, rows), (rows, L), (rows + L, L))[which]
        view = wg.at[plane(p), pl.ds(at, size), cols(t)]
        return remote(view, view, zs.at[which, p], zr.at[which, p], dp=d)

    for kind in (0, 1, 2):
        xy(kind, jnp.int32(0)).start()
    for p in range(1, NZ):
        j = zmod(d - offset(p))
        start(
            remote(
                w_ref.at[:, cols(j)], wg.at[d, pl.ds(0, rows), cols(t)], zs.at[0, p], zr.at[0, p], dp=j
            )
        )
        for k in range(2):
            start(
                remote(
                    kv_ref.at[k, cols(j), :],
                    wg.at[d, pl.ds(rows + L * k, L), cols(t)],
                    zs.at[1 + k, p],
                    zr.at[1 + k, p],
                    dp=j,
                )
            )

    embed = dot(pix[...], patch_w[...])
    centered = embed - jnp.mean(embed, -1, keepdims=True)
    inv_dev = lax.rsqrt(jnp.mean(centered * centered, -1, keepdims=True) + 1e-06)
    normalized = centered * inv_dev
    xhat[...] = normalized
    visual = (normalized * vgain[...]).astype(BF16)
    for s in range(NZ):
        j, h = s // 2, s % 2
        tok[d, s] = visual[j * slot : (j + 1) * slot, h * rows : (h + 1) * rows]

    def ring_gather(buf, send, recv, halves):
        def block(src, k, side):
            if k < NZ // 2:
                return buf.at[src]
            return buf.at[src, pl.ds(side * halves, halves)]

        def go(k):
            for side, sign in ((0, 1), (1, -1)):
                view = block(zmod(d - sign * (k - 1)), k, side)
                start(remote(view, view, send.at[side, k - 1], recv.at[side, k - 1], dp=zmod(d + sign)))

        def arrive(k):
            for side, sign in ((0, 1), (1, -1)):
                view = block(zmod(d - sign * k), k, side)
                remote(view, view, send.at[side, k - 1], recv.at[side, k - 1], dp=zmod(d + sign)).wait_recv()

        return go, arrive

    go, arrive = ring_gather(tok, as_, ar, NZ // 2)
    go(1)
    hid[...] = jnp.zeros_like(hid)

    def piece(p):
        s = plane(p)
        hid[...] += dot(tok[:, s].reshape(ntok, rows), wg[s, :rows, :])
        for k in range(2):
            kvl[k, cols(s), :] = wg[s, pl.ds(rows + L * k, L), :]

    def weights_step(i, carry):
        @pl.when(jnp.logical_and(i >= 1, i < NZ))
        def _():
            for which in range(3):
                z_in(i, which).wait_recv()
            for kind in (0, 1, 2):
                xy(kind, i).start()

        @pl.when(jnp.logical_and(i >= 1, i < NZ + 1))
        def _():
            xy(0, i - 1, True).wait_recv()
            xy(3, i - 1).start()
            xy(1, i - 1, True).wait_recv()
            xy(4, i - 1).start()
            xy(2, i - 1, True).wait_recv()
            xy(5, i - 1).start()
            xy(6, i - 1).start()

        @pl.when(jnp.logical_and(i >= 2, i < NZ + 2))
        def _():
            xy(3, i - 2, True).wait_recv()
            xy(4, i - 2, True).wait_recv()
            xy(7, i - 2).start()

        @pl.when(i >= 3)
        def _():
            for kind in (5, 6, 7):
                xy(kind, i - 3, True).wait_recv()
            piece(i - 3)

        return carry

    lax.fori_loop(1, 2, weights_step, 0)
    arrive(1)
    go(2)
    lax.fori_loop(2, 3, weights_step, 0)
    arrive(2)
    go(3)
    arrive(3)
    go(4)
    arrive(4)
    lax.fori_loop(3, NZ + 3, weights_step, 0)

    hidden = hid[...].astype(BF16).astype(F32)
    hid[...] = hidden
    gain = jnp.concatenate(
        [gain_ref[:, pl.ds(pl.multiple_of((b * NZ + d) * L, L), L)] for b in range(NT)], axis=-1
    )
    total_sq = jnp.sum(hidden * hidden, -1, keepdims=True)
    ssq_s[...] = jnp.broadcast_to(total_sq, (ntok, L)).reshape(NZ, slot, L)
    for r in range(1, NZ):
        j = zmod(d + r)
        start(remote(ssq_s.at[j], ssq_r.at[d], sqs.at[r], sqr.at[r], dp=j))
    ssq_r[d] = ssq_s[d]
    scaled = (hidden * gain).astype(BF16)
    for k in range(2):
        part1[:, k] = dot(scaled, kvl[k]).reshape(NZ, slot, NT * L)

    def ring_sum(part, sbuf, rbuf, send, recv, chunks, n):
        def copy(k, c, side):
            sign = 1 - 2 * side
            if k == 1:
                at = pl.ds((2 * c + side) * n, n)
            else:
                at = pl.ds(2 * c * n, 2 * n)
            return remote(
                sbuf.at[side, k - 1, at],
                rbuf.at[side, k - 1, at],
                send.at[side, k - 1, c],
                recv.at[side, k - 1, c],
                dp=zmod(d + sign),
            )

        def step(k, c):
            for side in (0, 1):
                sign = 1 - 2 * side
                e = zmod(d + sign * (NZ // 2 + 1 - k))
                if k > 1:
                    copy(k - 1, c, side).wait_recv()
                for b in range(2):
                    at = pl.ds((2 * c + b) * n, n)
                    if k == 1 and b != side:
                        continue
                    value = part[e, at]
                    if k > 2 or (k == 2 and b == side):
                        value = value + rbuf[side, k - 2, at].astype(F32)
                    sbuf[side, k - 1, at] = value.astype(BF16)
                start(copy(k, c, side))

        def result(c):
            at = pl.ds(2 * c * n, 2 * n)
            value = part[d, at]
            for side in (0, 1):
                copy(NZ // 2, c, side).wait_recv()
                value = value + rbuf[side, NZ // 2 - 1, at].astype(F32)
            return value

        return step, result

    step, result = ring_sum(part1, s1, r1, rs1s, rs1r, 1, 1)
    for k in range(1, NZ // 2 + 1):
        step(k, 0)
    for r in range(1, NZ):
        j = zmod(d - r)
        remote(ssq_s.at[j], ssq_r.at[j], sqs.at[r], sqr.at[r], dp=j).wait_recv()
    width = gain_ref.shape[1]
    root = lax.rsqrt(jnp.sum(ssq_r[...], axis=0) / width + 1e-06)[:, :1]
    pre = result(0)
    kvpre[...] = pre
    kvt[...] = (pre * root).astype(BF16)

    for r in range(1, NT):
        j = lax.rem(t + r, NT)
        start(remote(kvt.at[:, :, cols(j)], kvh.at[t], ats.at[r], atr.at[r], tensor=j))
    kvh[t] = kvt[:, :, cols(t)]
    heads = q_ref.shape[1] // L
    query = jnp.concatenate([q_ref[:, h * L : (h + 1) * L] for h in range(heads)], axis=0)
    masked = (cot_ref[...].astype(F32) * mask_ref[...].astype(F32)).astype(BF16)
    grad_out = jnp.concatenate([masked[:, h * L : (h + 1) * L] for h in range(heads)], axis=0)
    for r in range(1, NT):
        j = lax.rem(t + NT - r, NT)
        remote(kvh.at[j], kvh.at[j], ats.at[r], atr.at[r], tensor=j).wait_recv()
    scale = 1.0 / math.sqrt(L)
    keys = kvh[:, 0].reshape(ntok, L)
    values = kvh[:, 1].reshape(ntok, L)
    scores = dot_nt(keys, query) * scale
    e = jnp.exp(scores - jnp.max(scores, axis=0, keepdims=True))
    probs = e / jnp.sum(e, axis=0, keepdims=True)
    grad_probs = dot_nt(values, grad_out)
    inner = jnp.sum(probs * grad_probs, axis=0, keepdims=True)
    grad_scores = (probs * (grad_probs - inner) * scale).astype(BF16)
    gkvh[:, 0] = dot(grad_scores, query).astype(BF16).reshape(NT, slot, L)
    gkvh[:, 1] = dot(probs.astype(BF16), grad_out).astype(BF16).reshape(NT, slot, L)
    for r in range(1, NT):
        j = lax.rem(t + r, NT)
        start(remote(gkvh.at[j], gkv.at[d, :, :, cols(t)], bts.at[r], btr.at[r], tensor=j))
    gkv[d, :, :, cols(t)] = gkvh[t]
    for r in range(1, NT):
        j = lax.rem(t + NT - r, NT)
        remote(gkvh.at[j], gkv.at[d, :, :, cols(j)], bts.at[r], btr.at[r], tensor=j).wait_recv()

    go, arrive = ring_gather(gkv, ags, agr, 1)
    go(1)
    products = gkv[d].astype(F32) * kvpre[...]
    row_sum = jnp.sum(products[0] + products[1], -1, keepdims=True)
    coef = root * root * root * row_sum / width
    lane = lax.broadcasted_iota(jnp.int32, (slot, L), 1)
    scal[d] = jnp.where(lane < L // 2, root, coef)
    for r in range(1, NZ):
        start(remote(scal.at[d], scal.at[d], scs.at[r], scr.at[r], dp=zmod(d + r)))
    for k in range(1, NZ // 2):
        arrive(k)
        go(k + 1)
    arrive(NZ // 2)
    for r in range(1, NZ):
        j = zmod(d - r)
        remote(scal.at[j], scal.at[j], scs.at[r], scr.at[r], dp=j).wait_recv()
    grad_feat = dot_nt(gkv[:, 0].reshape(ntok, NT * L), kvl[0]) + dot_nt(
        gkv[:, 1].reshape(ntok, NT * L), kvl[1]
    )
    both = scal[...].reshape(ntok, L)
    grad_hidden = (both[:, :1] * gain * grad_feat - hid[...] * both[:, L - 1 :]).astype(BF16)

    chunks = NZ // 2
    step, result = ring_sum(part4, s4, r4, rs4s, rs4r, chunks, 1)
    for c in range(chunks):
        for b in range(2):
            s = 2 * c + b
            part4[:, s] = dot_nt(grad_hidden, wg[s, :rows, :]).reshape(NZ, slot, rows)
        step(1, c)
    for k in range(2, NZ // 2 + 1):
        for c in range(chunks):
            step(k, c)
    blocks = []
    for c in range(chunks):
        value = result(c)
        blocks.append(jnp.concatenate([value[0], value[1]], axis=-1))
    grad_visual = jnp.concatenate(blocks, axis=0)

    gain_grad = grad_visual * vgain[...]
    normalized = xhat[...]
    embed_grad = (
        inv_dev
        * (
            gain_grad
            - jnp.mean(gain_grad, -1, keepdims=True)
            - normalized * jnp.mean(gain_grad * normalized, -1, keepdims=True)
        )
    ).astype(BF16)
    gbuf[g] = dot_nt(embed_grad, patch_w[...]).astype(BF16)
    for r in range(1, ng):
        start(remote(gbuf.at[g], gbuf.at[g], grs.at[r], grr.at[r], group=lax.rem(g + r, ng)))
    for r in range(1, ng):
        j = lax.rem(g + ng - r, ng)
        remote(gbuf.at[j], gbuf.at[j], grs.at[r], grr.at[r], group=j).wait_recv()
    gradient = gbuf[0].astype(F32)
    for m in range(1, ng):
        gradient = gradient + gbuf[m].astype(F32)
    sqb[t] = jnp.broadcast_to(jnp.sum(gradient * gradient), (8, L))
    for r in range(1, NT):
        start(remote(sqb.at[t], sqb.at[t], fs.at[r], fr.at[r], tensor=lax.rem(t + r, NT)))
    for r in range(1, NT):
        j = lax.rem(t + NT - r, NT)
        remote(sqb.at[j], sqb.at[j], fs.at[r], fr.at[r], tensor=j).wait_recv()
    squares = jnp.sum(sqb[...], axis=0)[:1, :1]
    out_ref[...] = jnp.tanh(gradient * lax.rsqrt(squares / n_pixels + 1e-06))

    for copy in sent:
        copy.wait_send()

    def drain(p, carry):
        for kind in range(8):
            xy(kind, p).wait_send()
        return carry

    lax.fori_loop(0, NZ, drain, 0)


def body(
    images,
    step_size,
    member_mask,
    patch_weight,
    vision_norm_gain,
    merger_weight,
    norm_gain,
    kv_weight,
    queries,
    cotangent,
    *,
    ng,
):
    patches, pixels = images.shape[1:]
    slot = patches // 4
    rows, width = merger_weight.shape[1:]
    vwidth = patch_weight.shape[2]
    half = NZ // 2
    turned = images[0].reshape(slot, 4, pixels).transpose(1, 0, 2).reshape(patches, pixels)
    dma = pltpu.SemaphoreType.DMA
    vmem = pl.BlockSpec(memory_space=pltpu.VMEM)
    direction = pl.pallas_call(
        functools.partial(kernel, ng, float(NT * patches * pixels)),
        out_shape=jax.ShapeDtypeStruct((patches, pixels), F32),
        in_specs=[vmem] * 9,
        out_specs=vmem,
        scratch_shapes=[
            pltpu.VMEM((NZ, rows + 2 * L, NT * L), BF16),
            pltpu.VMEM((2, NZ * L, NT * L), BF16),
            pltpu.VMEM((NZ, NZ, slot, rows), BF16),
            pltpu.VMEM((NZ * slot, NT * L), F32),
            pltpu.VMEM((NZ, 2, slot, NT * L), F32),
            pltpu.VMEM((2, half, 2, slot, NT * L), BF16),
            pltpu.VMEM((2, half, 2, slot, NT * L), BF16),
            pltpu.VMEM((NZ, slot, L), F32),
            pltpu.VMEM((NZ, slot, L), F32),
            pltpu.VMEM((2, slot, NT * L), F32),
            pltpu.VMEM((2, slot, NT * L), BF16),
            pltpu.VMEM((NT, 2, slot, L), BF16),
            pltpu.VMEM((NT, 2, slot, L), BF16),
            pltpu.VMEM((NZ, 2, slot, NT * L), BF16),
            pltpu.VMEM((NZ, slot, L), F32),
            pltpu.VMEM((NZ, NZ, slot, rows), F32),
            pltpu.VMEM((2, half, NZ, slot, rows), BF16),
            pltpu.VMEM((2, half, NZ, slot, rows), BF16),
            pltpu.VMEM((patches, vwidth), F32),
            pltpu.VMEM((ng, patches, pixels), BF16),
            pltpu.VMEM((NT, 8, L), F32),
            dma((3,)),
            dma((3, NZ)),
            dma((3, NZ)),
            dma((8, NZ)),
            dma((8, NZ)),
            dma((2, half)),
            dma((2, half)),
            dma((2, half, 1)),
            dma((2, half, 1)),
            dma((NZ,)),
            dma((NZ,)),
            dma((NT,)),
            dma((NT,)),
            dma((NT,)),
            dma((NT,)),
            dma((2, half)),
            dma((2, half)),
            dma((NZ,)),
            dma((NZ,)),
            dma((2, half, half)),
            dma((2, half, half)),
            dma((max(ng, 2),)),
            dma((max(ng, 2),)),
            dma((NT,)),
            dma((NT,)),
        ],
        compiler_params=pltpu.CompilerParams(
            collective_id=0, has_side_effects=True, vmem_limit_bytes=60 * 1024 * 1024
        ),
    )(
        turned.astype(BF16),
        patch_weight[0],
        vision_norm_gain,
        merger_weight[0],
        norm_gain,
        kv_weight[0],
        queries[0, 0],
        cotangent[0, 0],
        member_mask,
    )
    direction = direction.reshape(4, slot, pixels).transpose(1, 0, 2).reshape(images.shape)
    adversarial = jnp.clip(images + step_size[:, None, None] * direction, 0.0, 1.0)
    return adversarial, direction


def solution(mesh):
    placed = (
        P("dp", "tensor", None),
        P("dp"),
        P("group", "dp"),
        P("group", None, None),
        P("group", None),
        P("group", "dp", "tensor"),
        P("group", None),
        P("group", None, "dp", "tensor"),
        P("group", "dp", None, "tensor"),
        P("group", "dp", None, "tensor"),
    )
    return jax.shard_map(
        functools.partial(body, ng=mesh.shape["group"]),
        mesh=mesh,
        in_specs=placed,
        out_specs=(P("dp", "tensor", None), P("dp", "tensor", None)),
        check_vma=False,
    )
```

```python
import functools
import math

import jax
import jax.numpy as jnp
from jax import lax
from jax.experimental import pallas as pl
from jax.experimental.pallas import tpu as pltpu
from jax.sharding import PartitionSpec as P

F32 = jnp.float32
BF16 = jnp.bfloat16
NZ = 8
NT = 8
NY = 4
L = 128
AHEAD = 3
STOPS = (3, 5, 7, 8)
LATE = 8
PART = 192
MESH = pl.DeviceIdType.MESH


def dot(a, b):
    return jnp.dot(a, b, preferred_element_type=F32)


def dot_nt(a, b):
    return lax.dot_general(a, b, (((1,), (1,)), ((), ())), preferred_element_type=F32)


def kernel(
    ng,
    n_pixels,
    pix,
    patch_w,
    vgain,
    w_ref,
    gain_ref,
    kv_ref,
    q_ref,
    cot_ref,
    mask_ref,
    out_ref,
    wg,
    kvl,
    tok,
    hid,
    part1,
    s1,
    r1,
    ssq_s,
    ssq_r,
    kvpre,
    kvt,
    kvh,
    gkvh,
    gkv,
    scal,
    part4,
    s4,
    r4,
    xhat,
    gbuf,
    sqb,
    local_sem,
    zs,
    zr,
    xs,
    xr,
    as_,
    ar,
    rs1s,
    rs1r,
    sqs,
    sqr,
    ats,
    atr,
    bts,
    btr,
    ags,
    agr,
    scs,
    scr,
    rs4s,
    rs4r,
    grs,
    grr,
    fs,
    fr,
):
    g = lax.axis_index("group")
    d = lax.axis_index("dp")
    t = lax.axis_index("tensor")
    x, y = t // NY, lax.rem(t, NY)
    rows = w_ref.shape[0]
    half_rows = (rows + 2 * L) // 2
    slot = tok.shape[2]
    ntok = NZ * slot

    def zmod(i):
        return lax.rem(i + 2 * NZ, NZ)

    def cols(i):
        return pl.ds(pl.multiple_of(i * L, L), L)

    def remote(src, dst, send, recv, **to):
        return pltpu.make_async_remote_copy(
            src_ref=src, dst_ref=dst, send_sem=send, recv_sem=recv, device_id=to, device_id_type=MESH
        )

    sent = []

    def start(copy):
        copy.start()
        sent.append(copy)

    barrier = pltpu.get_barrier_semaphore()
    for r in range(1, NZ):
        pl.semaphore_signal(barrier, inc=1, device_id={"dp": zmod(d + r)}, device_id_type=MESH)
    for r in range(1, NT):
        pl.semaphore_signal(barrier, inc=1, device_id={"tensor": lax.rem(t + r, NT)}, device_id_type=MESH)
    for r in range(1, ng):
        pl.semaphore_signal(barrier, inc=1, device_id={"group": lax.rem(g + r, ng)}, device_id_type=MESH)

    own = [
        pltpu.make_async_copy(w_ref.at[:, cols(d)], wg.at[d, pl.ds(0, rows), cols(t)], local_sem.at[0])
    ]
    for k in range(2):
        own.append(
            pltpu.make_async_copy(
                kv_ref.at[k, cols(d), :], wg.at[d, pl.ds(rows + L * k, L), cols(t)], local_sem.at[1 + k]
            )
        )
    for c in own:
        c.start()
    pl.semaphore_wait(barrier, NZ - 1 + NT - 1 + ng - 1)

    for c in own:
        c.wait()

    up = x * NY + lax.rem(y + 1, NY)
    down = x * NY + lax.rem(y + NY - 1, NY)
    far = x * NY + lax.rem(y + 2, NY)
    xo = (1 - x) * NY
    across = xo + y
    whole, lo, hi = (0, 2 * half_rows), (0, half_rows), (half_rows, half_rows)
    first, rest = (0, PART), (PART, 2 * half_rows - PART)
    kinds = (
        (t, up, down, whole),
        (t, down, up, whole),
        (t, across, across, whole),
        (down, up, far, lo),
        (up, down, far, hi),
        (across, up, xo + lax.rem(y + NY - 1, NY), rest),
        (across, down, xo + lax.rem(y + 1, NY), rest),
        (far, across, xo + lax.rem(y + 2, NY), whole),
        (up, across, xo + lax.rem(y + 1, NY), first),
        (down, across, xo + lax.rem(y + NY - 1, NY), first),
    )

    def plane(p):
        step = (p + 1) // 2
        return zmod(d + jnp.where(lax.rem(p, 2) == 1, step, -step))

    def xy(kind, p, incoming=False):
        block, to, arrives, (at, size) = kinds[kind]
        view = wg.at[plane(p), pl.ds(at, size), cols(arrives if incoming else block)]
        return remote(view, view, xs.at[kind, p], xr.at[kind, p], tensor=to)

    def z_in(p, which):
        at, size = ((0, rows), (rows, L), (rows + L, L))[which]
        view = wg.at[plane(p), pl.ds(at, size), cols(t)]
        return remote(view, view, zs.at[which, p], zr.at[which, p], dp=d)

    def z_out(p, which):
        step = (p + 1) // 2
        j = zmod(d + jnp.where(lax.rem(p, 2) == 1, -step, step))
        at, size = ((0, rows), (rows, L), (rows + L, L))[which]
        src = w_ref.at[:, cols(j)] if which == 0 else kv_ref.at[which - 1, cols(j), :]
        dst = wg.at[d, pl.ds(at, size), cols(t)]
        return remote(src, dst, zs.at[which, p], zr.at[which, p], dp=j)

    for kind in (0, 1, 2):
        xy(kind, jnp.int32(0)).start()
    for p in range(1, AHEAD + 1):
        for which in range(3):
            z_out(jnp.int32(p), which).start()

    embed = dot(pix[...], patch_w[...])
    centered = embed - jnp.mean(embed, -1, keepdims=True)
    inv_dev = lax.rsqrt(jnp.mean(centered * centered, -1, keepdims=True) + 1e-06)
    normalized = centered * inv_dev
    xhat[...] = normalized
    visual = (normalized * vgain[...]).astype(BF16)
    for s in range(NZ):
        j, h = s // 2, s % 2
        tok[d, s] = visual[j * slot : (j + 1) * slot, h * rows : (h + 1) * rows]

    def ring_gather(buf, send, recv, halves):
        def block(src, k, side):
            if k < NZ // 2:
                return buf.at[src]
            return buf.at[src, pl.ds(side * halves, halves)]

        def go(k):
            for side, sign in ((0, 1), (1, -1)):
                view = block(zmod(d - sign * (k - 1)), k, side)
                start(remote(view, view, send.at[side, k - 1], recv.at[side, k - 1], dp=zmod(d + sign)))

        def arrive(k):
            for side, sign in ((0, 1), (1, -1)):
                view = block(zmod(d - sign * k), k, side)
                remote(view, view, send.at[side, k - 1], recv.at[side, k - 1], dp=zmod(d + sign)).wait_recv()

        return go, arrive

    go, arrive = ring_gather(tok, as_, ar, NZ // 2)
    go(1)
    hid[...] = jnp.zeros_like(hid)

    def piece(p):
        s = plane(p)
        hid[...] += dot(tok[:, s].reshape(ntok, rows), wg[s, :rows, :])
        for k in range(2):
            kvl[k, cols(s), :] = wg[s, pl.ds(rows + L * k, L), :]

    def weights_step(i, carry):
        @pl.when(jnp.logical_and(i >= 1, i < NZ))
        def _():
            for which in range(3):
                z_in(i, which).wait_recv()
            for kind in (0, 1, 2):
                xy(kind, i).start()

        @pl.when(i + AHEAD < NZ)
        def _():
            for which in range(3):
                z_out(i + AHEAD, which).start()

        @pl.when(jnp.logical_and(i >= 1, i < NZ + 1))
        def _():
            xy(0, i - 1, True).wait_recv()
            xy(3, i - 1).start()
            xy(9, i - 1).start()
            xy(1, i - 1, True).wait_recv()
            xy(4, i - 1).start()
            xy(8, i - 1).start()
            xy(2, i - 1, True).wait_recv()
            xy(5, i - 1).start()
            xy(6, i - 1).start()

        @pl.when(jnp.logical_and(i >= 2, i < NZ + 2))
        def _():
            xy(3, i - 2, True).wait_recv()
            xy(4, i - 2, True).wait_recv()
            xy(7, i - 2).start()

        @pl.when(i >= 3)
        def _():
            for kind in (5, 6, 7, 8, 9):
                xy(kind, i - 3, True).wait_recv()

        @pl.when(i >= LATE)
        def _():
            piece(i - LATE)

        return carry

    at = 1
    for k, stop in enumerate(STOPS):
        lax.fori_loop(at, stop, weights_step, 0)
        arrive(k + 1)
        if k < 3:
            go(k + 2)
        at = stop
    lax.fori_loop(at, NZ + 3, weights_step, 0)
    lax.fori_loop(NZ + 3 - LATE, NZ, lambda p, carry: (piece(p), carry)[1], 0)

    hidden = hid[...].astype(BF16).astype(F32)
    hid[...] = hidden
    gain = jnp.concatenate(
        [gain_ref[:, pl.ds(pl.multiple_of((b * NZ + d) * L, L), L)] for b in range(NT)], axis=-1
    )
    total_sq = jnp.sum(hidden * hidden, -1, keepdims=True)
    ssq_s[...] = jnp.broadcast_to(total_sq, (ntok, L)).reshape(NZ, slot, L)
    for r in range(1, NZ):
        j = zmod(d + r)
        start(remote(ssq_s.at[j], ssq_r.at[d], sqs.at[r], sqr.at[r], dp=j))
    ssq_r[d] = ssq_s[d]
    scaled = (hidden * gain).astype(BF16)
    for k in range(2):
        part1[:, k] = dot(scaled, kvl[k]).reshape(NZ, slot, NT * L)

    def ring_sum(part, sbuf, rbuf, send, recv, chunks, n):
        def copy(k, c, side):
            sign = 1 - 2 * side
            if k == 1:
                at = pl.ds((2 * c + side) * n, n)
            else:
                at = pl.ds(2 * c * n, 2 * n)
            return remote(
                sbuf.at[side, k - 1, at],
                rbuf.at[side, k - 1, at],
                send.at[side, k - 1, c],
                recv.at[side, k - 1, c],
                dp=zmod(d + sign),
            )

        def step(k, c):
            for side in (0, 1):
                sign = 1 - 2 * side
                e = zmod(d + sign * (NZ // 2 + 1 - k))
                if k > 1:
                    copy(k - 1, c, side).wait_recv()
                for b in range(2):
                    at = pl.ds((2 * c + b) * n, n)
                    if k == 1 and b != side:
                        continue
                    value = part[e, at]
                    if k > 2 or (k == 2 and b == side):
                        value = value + rbuf[side, k - 2, at].astype(F32)
                    sbuf[side, k - 1, at] = value.astype(BF16)
                start(copy(k, c, side))

        def result(c):
            at = pl.ds(2 * c * n, 2 * n)
            value = part[d, at]
            for side in (0, 1):
                copy(NZ // 2, c, side).wait_recv()
                value = value + rbuf[side, NZ // 2 - 1, at].astype(F32)
            return value

        return step, result

    step, result = ring_sum(part1, s1, r1, rs1s, rs1r, 1, 1)
    for k in range(1, NZ // 2 + 1):
        step(k, 0)
    for r in range(1, NZ):
        j = zmod(d - r)
        remote(ssq_s.at[j], ssq_r.at[j], sqs.at[r], sqr.at[r], dp=j).wait_recv()
    width = gain_ref.shape[1]
    root = lax.rsqrt(jnp.sum(ssq_r[...], axis=0) / width + 1e-06)[:, :1]
    pre = result(0)
    kvpre[...] = pre
    kvt[...] = (pre * root).astype(BF16)

    for r in range(1, NT):
        j = lax.rem(t + r, NT)
        start(remote(kvt.at[:, :, cols(j)], kvh.at[t], ats.at[r], atr.at[r], tensor=j))
    kvh[t] = kvt[:, :, cols(t)]
    heads = q_ref.shape[1] // L
    query = jnp.concatenate([q_ref[:, h * L : (h + 1) * L] for h in range(heads)], axis=0)
    masked = (cot_ref[...].astype(F32) * mask_ref[...].astype(F32)).astype(BF16)
    grad_out = jnp.concatenate([masked[:, h * L : (h + 1) * L] for h in range(heads)], axis=0)
    for r in range(1, NT):
        j = lax.rem(t + NT - r, NT)
        remote(kvh.at[j], kvh.at[j], ats.at[r], atr.at[r], tensor=j).wait_recv()
    scale = 1.0 / math.sqrt(L)
    keys = kvh[:, 0].reshape(ntok, L)
    values = kvh[:, 1].reshape(ntok, L)
    scores = dot_nt(keys, query) * scale
    e = jnp.exp(scores - jnp.max(scores, axis=0, keepdims=True))
    probs = e / jnp.sum(e, axis=0, keepdims=True)
    grad_probs = dot_nt(values, grad_out)
    inner = jnp.sum(probs * grad_probs, axis=0, keepdims=True)
    grad_scores = (probs * (grad_probs - inner) * scale).astype(BF16)
    gkvh[:, 0] = dot(grad_scores, query).astype(BF16).reshape(NT, slot, L)
    gkvh[:, 1] = dot(probs.astype(BF16), grad_out).astype(BF16).reshape(NT, slot, L)
    for r in range(1, NT):
        j = lax.rem(t + r, NT)
        start(remote(gkvh.at[j], gkv.at[d, :, :, cols(t)], bts.at[r], btr.at[r], tensor=j))
    gkv[d, :, :, cols(t)] = gkvh[t]
    for r in range(1, NT):
        j = lax.rem(t + NT - r, NT)
        remote(gkvh.at[j], gkv.at[d, :, :, cols(j)], bts.at[r], btr.at[r], tensor=j).wait_recv()

    go, arrive = ring_gather(gkv, ags, agr, 1)
    go(1)
    products = gkv[d].astype(F32) * kvpre[...]
    row_sum = jnp.sum(products[0] + products[1], -1, keepdims=True)
    coef = root * root * root * row_sum / width
    lane = lax.broadcasted_iota(jnp.int32, (slot, L), 1)
    scal[d] = jnp.where(lane < L // 2, root, coef)
    for r in range(1, NZ):
        start(remote(scal.at[d], scal.at[d], scs.at[r], scr.at[r], dp=zmod(d + r)))
    for k in range(1, NZ // 2):
        arrive(k)
        go(k + 1)
    arrive(NZ // 2)
    for r in range(1, NZ):
        j = zmod(d - r)
        remote(scal.at[j], scal.at[j], scs.at[r], scr.at[r], dp=j).wait_recv()
    grad_feat = dot_nt(gkv[:, 0].reshape(ntok, NT * L), kvl[0]) + dot_nt(
        gkv[:, 1].reshape(ntok, NT * L), kvl[1]
    )
    both = scal[...].reshape(ntok, L)
    grad_hidden = (both[:, :1] * gain * grad_feat - hid[...] * both[:, L - 1 :]).astype(BF16)

    chunks = NZ // 2
    step, result = ring_sum(part4, s4, r4, rs4s, rs4r, chunks, 1)
    for c in range(chunks):
        for b in range(2):
            s = 2 * c + b
            part4[:, s] = dot_nt(grad_hidden, wg[s, :rows, :]).reshape(NZ, slot, rows)
        step(1, c)
    for k in range(2, NZ // 2 + 1):
        for c in range(chunks):
            step(k, c)
    blocks = []
    for c in range(chunks):
        value = result(c)
        blocks.append(jnp.concatenate([value[0], value[1]], axis=-1))
    grad_visual = jnp.concatenate(blocks, axis=0)

    gain_grad = grad_visual * vgain[...]
    normalized = xhat[...]
    embed_grad = (
        inv_dev
        * (
            gain_grad
            - jnp.mean(gain_grad, -1, keepdims=True)
            - normalized * jnp.mean(gain_grad * normalized, -1, keepdims=True)
        )
    ).astype(BF16)
    gbuf[g] = dot_nt(embed_grad, patch_w[...]).astype(BF16)
    for r in range(1, ng):
        start(remote(gbuf.at[g], gbuf.at[g], grs.at[r], grr.at[r], group=lax.rem(g + r, ng)))
    for r in range(1, ng):
        j = lax.rem(g + ng - r, ng)
        remote(gbuf.at[j], gbuf.at[j], grs.at[r], grr.at[r], group=j).wait_recv()
    gradient = gbuf[0].astype(F32)
    for m in range(1, ng):
        gradient = gradient + gbuf[m].astype(F32)
    sqb[t] = jnp.broadcast_to(jnp.sum(gradient * gradient), (8, L))
    for r in range(1, NT):
        start(remote(sqb.at[t], sqb.at[t], fs.at[r], fr.at[r], tensor=lax.rem(t + r, NT)))
    for r in range(1, NT):
        j = lax.rem(t + NT - r, NT)
        remote(sqb.at[j], sqb.at[j], fs.at[r], fr.at[r], tensor=j).wait_recv()
    squares = jnp.sum(sqb[...], axis=0)[:1, :1]
    out_ref[...] = jnp.tanh(gradient * lax.rsqrt(squares / n_pixels + 1e-06))

    for copy in sent:
        copy.wait_send()

    def drain(p, carry):
        for kind in range(len(kinds)):
            xy(kind, p).wait_send()

        @pl.when(p > 0)
        def _():
            for which in range(3):
                z_out(p, which).wait_send()

        return carry

    lax.fori_loop(0, NZ, drain, 0)


def body(
    images,
    step_size,
    member_mask,
    patch_weight,
    vision_norm_gain,
    merger_weight,
    norm_gain,
    kv_weight,
    queries,
    cotangent,
    *,
    ng,
):
    patches, pixels = images.shape[1:]
    slot = patches // 4
    rows, width = merger_weight.shape[1:]
    vwidth = patch_weight.shape[2]
    half = NZ // 2
    turned = images[0].reshape(slot, 4, pixels).transpose(1, 0, 2).reshape(patches, pixels)
    dma = pltpu.SemaphoreType.DMA
    vmem = pl.BlockSpec(memory_space=pltpu.VMEM)
    direction = pl.pallas_call(
        functools.partial(kernel, ng, float(NT * patches * pixels)),
        out_shape=jax.ShapeDtypeStruct((patches, pixels), F32),
        in_specs=[vmem] * 9,
        out_specs=vmem,
        scratch_shapes=[
            pltpu.VMEM((NZ, rows + 2 * L, NT * L), BF16),
            pltpu.VMEM((2, NZ * L, NT * L), BF16),
            pltpu.VMEM((NZ, NZ, slot, rows), BF16),
            pltpu.VMEM((NZ * slot, NT * L), F32),
            pltpu.VMEM((NZ, 2, slot, NT * L), F32),
            pltpu.VMEM((2, half, 2, slot, NT * L), BF16),
            pltpu.VMEM((2, half, 2, slot, NT * L), BF16),
            pltpu.VMEM((NZ, slot, L), F32),
            pltpu.VMEM((NZ, slot, L), F32),
            pltpu.VMEM((2, slot, NT * L), F32),
            pltpu.VMEM((2, slot, NT * L), BF16),
            pltpu.VMEM((NT, 2, slot, L), BF16),
            pltpu.VMEM((NT, 2, slot, L), BF16),
            pltpu.VMEM((NZ, 2, slot, NT * L), BF16),
            pltpu.VMEM((NZ, slot, L), F32),
            pltpu.VMEM((NZ, NZ, slot, rows), F32),
            pltpu.VMEM((2, half, NZ, slot, rows), BF16),
            pltpu.VMEM((2, half, NZ, slot, rows), BF16),
            pltpu.VMEM((patches, vwidth), F32),
            pltpu.VMEM((ng, patches, pixels), BF16),
            pltpu.VMEM((NT, 8, L), F32),
            dma((3,)),
            dma((3, NZ)),
            dma((3, NZ)),
            dma((10, NZ)),
            dma((10, NZ)),
            dma((2, half)),
            dma((2, half)),
            dma((2, half, 1)),
            dma((2, half, 1)),
            dma((NZ,)),
            dma((NZ,)),
            dma((NT,)),
            dma((NT,)),
            dma((NT,)),
            dma((NT,)),
            dma((2, half)),
            dma((2, half)),
            dma((NZ,)),
            dma((NZ,)),
            dma((2, half, half)),
            dma((2, half, half)),
            dma((max(ng, 2),)),
            dma((max(ng, 2),)),
            dma((NT,)),
            dma((NT,)),
        ],
        compiler_params=pltpu.CompilerParams(
            collective_id=0, has_side_effects=True, vmem_limit_bytes=60 * 1024 * 1024
        ),
    )(
        turned.astype(BF16),
        patch_weight[0],
        vision_norm_gain,
        merger_weight[0],
        norm_gain,
        kv_weight[0],
        queries[0, 0],
        cotangent[0, 0],
        member_mask,
    )
    direction = direction.reshape(4, slot, pixels).transpose(1, 0, 2).reshape(images.shape)
    adversarial = jnp.clip(images + step_size[:, None, None] * direction, 0.0, 1.0)
    return adversarial, direction


def solution(mesh):
    placed = (
        P("dp", "tensor", None),
        P("dp"),
        P("group", "dp"),
        P("group", None, None),
        P("group", None),
        P("group", "dp", "tensor"),
        P("group", None),
        P("group", None, "dp", "tensor"),
        P("group", "dp", None, "tensor"),
        P("group", "dp", None, "tensor"),
    )
    return jax.shard_map(
        functools.partial(body, ng=mesh.shape["group"]),
        mesh=mesh,
        in_specs=placed,
        out_specs=(P("dp", "tensor", None), P("dp", "tensor", None)),
        check_vma=False,
    )
```

```python
import functools
import math

import jax
import jax.numpy as jnp
from jax import lax
from jax.experimental import pallas as pl
from jax.experimental.pallas import tpu as pltpu
from jax.sharding import PartitionSpec as P

F32 = jnp.float32
BF16 = jnp.bfloat16
NZ = 8
NT = 8
NY = 4
L = 128
AHEAD = 3
STOPS = (3, 5, 7, 8)
PART = 192
MESH = pl.DeviceIdType.MESH


def dot(a, b):
    return jnp.dot(a, b, preferred_element_type=F32)


def dot_nt(a, b):
    return lax.dot_general(a, b, (((1,), (1,)), ((), ())), preferred_element_type=F32)


def kernel(
    ng,
    n_pixels,
    pix,
    patch_hbm,
    vgain,
    w_ref,
    gain_ref,
    kv_ref,
    q_ref,
    cot_ref,
    mask_ref,
    out_ref,
    wg,
    kvl,
    tok,
    hid,
    part1,
    s1,
    r1,
    ssq_s,
    ssq_r,
    kvpre,
    kvt,
    kvh,
    gkvh,
    gkv,
    scal,
    part4,
    s4,
    r4,
    xhat,
    gbuf,
    sqb,
    patch_w,
    local_sem,
    zs,
    zr,
    xs,
    xr,
    as_,
    ar,
    rs1s,
    rs1r,
    sqs,
    sqr,
    ats,
    atr,
    bts,
    btr,
    ags,
    agr,
    scs,
    scr,
    rs4s,
    rs4r,
    grs,
    grr,
    fs,
    fr,
):
    g = lax.axis_index("group")
    d = lax.axis_index("dp")
    t = lax.axis_index("tensor")
    x, y = t // NY, lax.rem(t, NY)
    rows = w_ref.shape[0]
    half_rows = (rows + 2 * L) // 2
    slot = tok.shape[2]
    ntok = NZ * slot

    def zmod(i):
        return lax.rem(i + 2 * NZ, NZ)

    def cols(i):
        return pl.ds(pl.multiple_of(i * L, L), L)

    def remote(src, dst, send, recv, **to):
        return pltpu.make_async_remote_copy(
            src_ref=src, dst_ref=dst, send_sem=send, recv_sem=recv, device_id=to, device_id_type=MESH
        )

    sent = []

    def start(copy):
        copy.start()
        sent.append(copy)

    load_patch = pltpu.make_async_copy(patch_hbm, patch_w, local_sem.at[3])
    load_patch.start()
    barrier = pltpu.get_barrier_semaphore()
    for r in range(1, NZ):
        pl.semaphore_signal(barrier, inc=1, device_id={"dp": zmod(d + r)}, device_id_type=MESH)
    for r in range(1, NT):
        pl.semaphore_signal(barrier, inc=1, device_id={"tensor": lax.rem(t + r, NT)}, device_id_type=MESH)
    for r in range(1, ng):
        pl.semaphore_signal(barrier, inc=1, device_id={"group": lax.rem(g + r, ng)}, device_id_type=MESH)

    own = [
        pltpu.make_async_copy(w_ref.at[:, cols(d)], wg.at[d, pl.ds(0, rows), cols(t)], local_sem.at[0])
    ]
    for k in range(2):
        own.append(
            pltpu.make_async_copy(
                kv_ref.at[k, cols(d), :], wg.at[d, pl.ds(rows + L * k, L), cols(t)], local_sem.at[1 + k]
            )
        )
    for c in own:
        c.start()
    pl.semaphore_wait(barrier, NZ - 1 + NT - 1 + ng - 1)

    for c in own:
        c.wait()

    up = x * NY + lax.rem(y + 1, NY)
    down = x * NY + lax.rem(y + NY - 1, NY)
    far = x * NY + lax.rem(y + 2, NY)
    xo = (1 - x) * NY
    across = xo + y
    whole, lo, hi = (0, 2 * half_rows), (0, half_rows), (half_rows, half_rows)
    first, rest = (0, PART), (PART, 2 * half_rows - PART)
    kinds = (
        (t, up, down, whole),
        (t, down, up, whole),
        (t, across, across, whole),
        (down, up, far, lo),
        (up, down, far, hi),
        (across, up, xo + lax.rem(y + NY - 1, NY), rest),
        (across, down, xo + lax.rem(y + 1, NY), rest),
        (far, across, xo + lax.rem(y + 2, NY), whole),
        (up, across, xo + lax.rem(y + 1, NY), first),
        (down, across, xo + lax.rem(y + NY - 1, NY), first),
    )

    def plane(p):
        step = (p + 1) // 2
        return zmod(d + jnp.where(lax.rem(p, 2) == 1, step, -step))

    def xy(kind, p, incoming=False):
        block, to, arrives, (at, size) = kinds[kind]
        view = wg.at[plane(p), pl.ds(at, size), cols(arrives if incoming else block)]
        return remote(view, view, xs.at[kind, p], xr.at[kind, p], tensor=to)

    def z_in(p, which):
        at, size = ((0, rows), (rows, L), (rows + L, L))[which]
        view = wg.at[plane(p), pl.ds(at, size), cols(t)]
        return remote(view, view, zs.at[which, p], zr.at[which, p], dp=d)

    def z_out(p, which):
        step = (p + 1) // 2
        j = zmod(d + jnp.where(lax.rem(p, 2) == 1, -step, step))
        at, size = ((0, rows), (rows, L), (rows + L, L))[which]
        src = w_ref.at[:, cols(j)] if which == 0 else kv_ref.at[which - 1, cols(j), :]
        dst = wg.at[d, pl.ds(at, size), cols(t)]
        return remote(src, dst, zs.at[which, p], zr.at[which, p], dp=j)

    for kind in (0, 1, 2):
        xy(kind, jnp.int32(0)).start()
    for p in range(1, AHEAD + 1):
        for which in range(3):
            z_out(jnp.int32(p), which).start()

    load_patch.wait()
    embed = dot(pix[...], patch_w[...])
    centered = embed - jnp.mean(embed, -1, keepdims=True)
    inv_dev = lax.rsqrt(jnp.mean(centered * centered, -1, keepdims=True) + 1e-06)
    normalized = centered * inv_dev
    xhat[...] = normalized
    visual = (normalized * vgain[...]).astype(BF16)
    for s in range(NZ):
        j, h = s // 2, s % 2
        tok[d, s] = visual[j * slot : (j + 1) * slot, h * rows : (h + 1) * rows]

    def ring_gather(buf, send, recv, views):
        n = len(views)

        def copy(src, k, side, c):
            view = buf.at[(src,) + views[c]]
            to = zmod(d + 1 - 2 * side)
            return remote(view, view, send.at[side, k - 1, c], recv.at[side, k - 1, c], dp=to)

        def order(k, side):
            own_half = list(range(side * n // 2, (side + 1) * n // 2))
            return own_half if k == NZ // 2 else own_half + [c for c in range(n) if c not in own_half]

        def go(k):
            for i in range(n):
                for side in (0, 1):
                    if i < len(order(k, side)):
                        start(copy(zmod(d - (1 - 2 * side) * (k - 1)), k, side, order(k, side)[i]))

        def arrive(k, then_go=False):
            for i in range(n):
                for side in (0, 1):
                    if i < len(order(k, side)):
                        src, c = zmod(d - (1 - 2 * side) * k), order(k, side)[i]
                        copy(src, k, side, c).wait_recv()
                        if then_go and c in order(k + 1, side):
                            start(copy(src, k + 1, side, c))

        return go, arrive

    go, arrive = ring_gather(tok, as_, ar, [(pl.ds(0, NZ // 2),), (pl.ds(NZ // 2, NZ // 2),)])
    go(1)
    hid[...] = jnp.zeros_like(hid)

    def piece(p, carry):
        s = plane(p)
        hid[...] += dot(tok[:, s].reshape(ntok, rows), wg[s, :rows, :])
        for k in range(2):
            kvl[k, cols(s), :] = wg[s, pl.ds(rows + L * k, L), :]
        return carry

    def pieces(start_at, stop_at):
        lax.fori_loop(start_at, stop_at, piece, 0)

    def weights_step(i, carry):
        @pl.when(jnp.logical_and(i >= 1, i < NZ))
        def _():
            for which in range(3):
                z_in(i, which).wait_recv()
            for kind in (0, 1, 2):
                xy(kind, i).start()

        @pl.when(i + AHEAD < NZ)
        def _():
            for which in range(3):
                z_out(i + AHEAD, which).start()

        @pl.when(jnp.logical_and(i >= 1, i < NZ + 1))
        def _():
            xy(0, i - 1, True).wait_recv()
            xy(3, i - 1).start()
            xy(9, i - 1).start()
            xy(1, i - 1, True).wait_recv()
            xy(4, i - 1).start()
            xy(8, i - 1).start()
            xy(2, i - 1, True).wait_recv()
            xy(5, i - 1).start()
            xy(6, i - 1).start()

        @pl.when(jnp.logical_and(i >= 2, i < NZ + 2))
        def _():
            xy(3, i - 2, True).wait_recv()
            xy(4, i - 2, True).wait_recv()
            xy(7, i - 2).start()

        @pl.when(i >= NZ)
        def _():
            first_piece = 3 * (i - NZ)
            pieces(first_piece, jnp.minimum(first_piece + 3, NZ - 1))

        @pl.when(i >= 3)
        def _():
            for kind in (5, 6, 7, 8, 9):
                xy(kind, i - 3, True).wait_recv()

        return carry

    at = 1
    for k, stop in enumerate(STOPS):
        lax.fori_loop(at, stop, weights_step, 0)
        arrive(k + 1, k < 3)
        at = stop
    lax.fori_loop(at, NZ + 3, weights_step, 0)
    pieces(NZ - 1, NZ)

    hidden = hid[...].astype(BF16).astype(F32)
    hid[...] = hidden
    gain = jnp.concatenate(
        [gain_ref[:, pl.ds(pl.multiple_of((b * NZ + d) * L, L), L)] for b in range(NT)], axis=-1
    )
    total_sq = jnp.sum(hidden * hidden, -1, keepdims=True)
    ssq_s[...] = jnp.broadcast_to(total_sq, (ntok, L)).reshape(NZ, slot, L)
    for r in range(1, NZ):
        j = zmod(d + r)
        start(remote(ssq_s.at[j], ssq_r.at[d], sqs.at[r], sqr.at[r], dp=j))
    ssq_r[d] = ssq_s[d]
    scaled = (hidden * gain).astype(BF16)
    def ring_sum(part, sbuf, rbuf, send, recv, chunks, n):
        def copy(k, c, side):
            sign = 1 - 2 * side
            if k == 1:
                at = pl.ds((2 * c + side) * n, n)
            else:
                at = pl.ds(2 * c * n, 2 * n)
            return remote(
                sbuf.at[side, k - 1, at],
                rbuf.at[side, k - 1, at],
                send.at[side, k - 1, c],
                recv.at[side, k - 1, c],
                dp=zmod(d + sign),
            )

        def step(k, c):
            for side in (0, 1):
                sign = 1 - 2 * side
                e = zmod(d + sign * (NZ // 2 + 1 - k))
                if k > 1:
                    copy(k - 1, c, side).wait_recv()
                for b in range(2):
                    at = pl.ds((2 * c + b) * n, n)
                    if k == 1 and b != side:
                        continue
                    value = part[e, at]
                    if k > 2 or (k == 2 and b == side):
                        value = value + rbuf[side, k - 2, at].astype(F32)
                    sbuf[side, k - 1, at] = value.astype(BF16)
                start(copy(k, c, side))

        def result(c):
            at = pl.ds(2 * c * n, 2 * n)
            value = part[d, at]
            for side in (0, 1):
                copy(NZ // 2, c, side).wait_recv()
                value = value + rbuf[side, NZ // 2 - 1, at].astype(F32)
            return value

        return step, result

    chunks = NZ // 2
    step, result = ring_sum(part1, s1, r1, rs1s, rs1r, chunks, 1)
    for c in range(chunks):
        at = c % 2 * 4 * L
        share = dot(scaled, kvl[c // 2, :, at : at + 4 * L])
        for b in range(2):
            part1[:, 2 * c + b] = share[:, 2 * b * L : 2 * (b + 1) * L].reshape(NZ, slot, 2 * L)
        step(1, c)
    for k in range(2, NZ // 2 + 1):
        for c in range(chunks):
            step(k, c)
    for r in range(1, NZ):
        j = zmod(d - r)
        remote(ssq_s.at[j], ssq_r.at[j], sqs.at[r], sqr.at[r], dp=j).wait_recv()
    width = gain_ref.shape[1]
    root = lax.rsqrt(jnp.sum(ssq_r[...], axis=0) / width + 1e-06)[:, :1]
    for c in range(chunks):
        pre = result(c)
        for b in range(2):
            at = (c % 2 * 2 + b) * 2 * L
            kvpre[c // 2, :, at : at + 2 * L] = pre[b]
            kvt[c // 2, :, at : at + 2 * L] = (pre[b] * root).astype(BF16)

    for r in range(1, NT):
        j = lax.rem(t + r, NT)
        start(remote(kvt.at[:, :, cols(j)], kvh.at[t], ats.at[r], atr.at[r], tensor=j))
    kvh[t] = kvt[:, :, cols(t)]
    heads = q_ref.shape[1] // L
    query = jnp.concatenate([q_ref[:, h * L : (h + 1) * L] for h in range(heads)], axis=0)
    masked = (cot_ref[...].astype(F32) * mask_ref[...].astype(F32)).astype(BF16)
    grad_out = jnp.concatenate([masked[:, h * L : (h + 1) * L] for h in range(heads)], axis=0)
    for r in range(1, NT):
        j = lax.rem(t + NT - r, NT)
        remote(kvh.at[j], kvh.at[j], ats.at[r], atr.at[r], tensor=j).wait_recv()
    scale = 1.0 / math.sqrt(L)
    keys = kvh[:, 0].reshape(ntok, L)
    values = kvh[:, 1].reshape(ntok, L)
    scores = dot_nt(keys, query) * scale
    e = jnp.exp(scores - jnp.max(scores, axis=0, keepdims=True))
    probs = e / jnp.sum(e, axis=0, keepdims=True)
    grad_probs = dot_nt(values, grad_out)
    inner = jnp.sum(probs * grad_probs, axis=0, keepdims=True)
    grad_scores = (probs * (grad_probs - inner) * scale).astype(BF16)
    gkvh[:, 0] = dot(grad_scores, query).astype(BF16).reshape(NT, slot, L)
    gkvh[:, 1] = dot(probs.astype(BF16), grad_out).astype(BF16).reshape(NT, slot, L)
    for r in range(1, NT):
        j = lax.rem(t + r, NT)
        start(remote(gkvh.at[j], gkv.at[d, :, :, cols(t)], bts.at[r], btr.at[r], tensor=j))
    gkv[d, :, :, cols(t)] = gkvh[t]
    for r in range(1, NT):
        j = lax.rem(t + NT - r, NT)
        remote(gkvh.at[j], gkv.at[d, :, :, cols(j)], bts.at[r], btr.at[r], tensor=j).wait_recv()

    spans = [(k, slice(None), pl.ds(h * 4 * L, 4 * L)) for k in range(2) for h in range(2)]
    go, arrive = ring_gather(gkv, ags, agr, spans)
    go(1)
    products = gkv[d].astype(F32) * kvpre[...]
    row_sum = jnp.sum(products[0] + products[1], -1, keepdims=True)
    coef = root * root * root * row_sum / width
    lane = lax.broadcasted_iota(jnp.int32, (slot, L), 1)
    scal[d] = jnp.where(lane < L // 2, root, coef)
    for r in range(1, NZ):
        start(remote(scal.at[d], scal.at[d], scs.at[r], scr.at[r], dp=zmod(d + r)))
    for k in range(1, NZ // 2):
        arrive(k, True)
    arrive(NZ // 2)
    for r in range(1, NZ):
        j = zmod(d - r)
        remote(scal.at[j], scal.at[j], scs.at[r], scr.at[r], dp=j).wait_recv()
    grad_feat = dot_nt(gkv[:, 0].reshape(ntok, NT * L), kvl[0]) + dot_nt(
        gkv[:, 1].reshape(ntok, NT * L), kvl[1]
    )
    both = scal[...].reshape(ntok, L)
    grad_hidden = (both[:, :1] * gain * grad_feat - hid[...] * both[:, L - 1 :]).astype(BF16)

    step, result = ring_sum(part4, s4, r4, rs4s, rs4r, chunks, 1)
    for c in range(chunks):
        for b in range(2):
            s = 2 * c + b
            part4[:, s] = dot_nt(grad_hidden, wg[s, :rows, :]).reshape(NZ, slot, rows)
        step(1, c)
    for k in range(2, NZ // 2 + 1):
        for c in range(chunks):
            step(k, c)
    blocks = []
    for c in range(chunks):
        value = result(c)
        blocks.append(jnp.concatenate([value[0], value[1]], axis=-1))
    grad_visual = jnp.concatenate(blocks, axis=0)

    gain_grad = grad_visual * vgain[...]
    normalized = xhat[...]
    embed_grad = (
        inv_dev
        * (
            gain_grad
            - jnp.mean(gain_grad, -1, keepdims=True)
            - normalized * jnp.mean(gain_grad * normalized, -1, keepdims=True)
        )
    ).astype(BF16)
    gbuf[g] = dot_nt(embed_grad, patch_w[...]).astype(BF16)
    for r in range(1, ng):
        start(remote(gbuf.at[g], gbuf.at[g], grs.at[r], grr.at[r], group=lax.rem(g + r, ng)))
    for r in range(1, ng):
        j = lax.rem(g + ng - r, ng)
        remote(gbuf.at[j], gbuf.at[j], grs.at[r], grr.at[r], group=j).wait_recv()
    gradient = gbuf[0].astype(F32)
    for m in range(1, ng):
        gradient = gradient + gbuf[m].astype(F32)
    sqb[t] = jnp.broadcast_to(jnp.sum(gradient * gradient), (8, L))
    for r in range(1, NT):
        start(remote(sqb.at[t], sqb.at[t], fs.at[r], fr.at[r], tensor=lax.rem(t + r, NT)))
    for r in range(1, NT):
        j = lax.rem(t + NT - r, NT)
        remote(sqb.at[j], sqb.at[j], fs.at[r], fr.at[r], tensor=j).wait_recv()
    squares = jnp.sum(sqb[...], axis=0)[:1, :1]
    out_ref[...] = jnp.tanh(gradient * lax.rsqrt(squares / n_pixels + 1e-06))

    for copy in sent:
        copy.wait_send()

    def drain(p, carry):
        for kind in range(len(kinds)):
            xy(kind, p).wait_send()

        @pl.when(p > 0)
        def _():
            for which in range(3):
                z_out(p, which).wait_send()

        return carry

    lax.fori_loop(0, NZ, drain, 0)


def body(
    images,
    step_size,
    member_mask,
    patch_weight,
    vision_norm_gain,
    merger_weight,
    norm_gain,
    kv_weight,
    queries,
    cotangent,
    *,
    ng,
):
    patches, pixels = images.shape[1:]
    slot = patches // 4
    rows, width = merger_weight.shape[1:]
    vwidth = patch_weight.shape[2]
    half = NZ // 2
    turned = images[0].reshape(slot, 4, pixels).transpose(1, 0, 2).reshape(patches, pixels)
    dma = pltpu.SemaphoreType.DMA
    vmem = pl.BlockSpec(memory_space=pltpu.VMEM)
    anywhere = pl.BlockSpec(memory_space=pl.ANY)
    direction = pl.pallas_call(
        functools.partial(kernel, ng, float(NT * patches * pixels)),
        out_shape=jax.ShapeDtypeStruct((patches, pixels), F32),
        in_specs=[vmem, anywhere, vmem, anywhere, vmem, anywhere, vmem, vmem, vmem],
        out_specs=vmem,
        scratch_shapes=[
            pltpu.VMEM((NZ, rows + 2 * L, NT * L), BF16),
            pltpu.VMEM((2, NZ * L, NT * L), BF16),
            pltpu.VMEM((NZ, NZ, slot, rows), BF16),
            pltpu.VMEM((NZ * slot, NT * L), F32),
            pltpu.VMEM((NZ, NZ, slot, 2 * L), F32),
            pltpu.VMEM((2, half, NZ, slot, 2 * L), BF16),
            pltpu.VMEM((2, half, NZ, slot, 2 * L), BF16),
            pltpu.VMEM((NZ, slot, L), F32),
            pltpu.VMEM((NZ, slot, L), F32),
            pltpu.VMEM((2, slot, NT * L), F32),
            pltpu.VMEM((2, slot, NT * L), BF16),
            pltpu.VMEM((NT, 2, slot, L), BF16),
            pltpu.VMEM((NT, 2, slot, L), BF16),
            pltpu.VMEM((NZ, 2, slot, NT * L), BF16),
            pltpu.VMEM((NZ, slot, L), F32),
            pltpu.VMEM((NZ, NZ, slot, rows), F32),
            pltpu.VMEM((2, half, NZ, slot, rows), BF16),
            pltpu.VMEM((2, half, NZ, slot, rows), BF16),
            pltpu.VMEM((patches, vwidth), F32),
            pltpu.VMEM((ng, patches, pixels), BF16),
            pltpu.VMEM((NT, 8, L), F32),
            pltpu.VMEM((pixels, vwidth), BF16),
            dma((4,)),
            dma((3, NZ)),
            dma((3, NZ)),
            dma((10, NZ)),
            dma((10, NZ)),
            dma((2, half, 2)),
            dma((2, half, 2)),
            dma((2, half, half)),
            dma((2, half, half)),
            dma((NZ,)),
            dma((NZ,)),
            dma((NT,)),
            dma((NT,)),
            dma((NT,)),
            dma((NT,)),
            dma((2, half, half)),
            dma((2, half, half)),
            dma((NZ,)),
            dma((NZ,)),
            dma((2, half, half)),
            dma((2, half, half)),
            dma((max(ng, 2),)),
            dma((max(ng, 2),)),
            dma((NT,)),
            dma((NT,)),
        ],
        compiler_params=pltpu.CompilerParams(
            collective_id=0, has_side_effects=True, vmem_limit_bytes=60 * 1024 * 1024
        ),
    )(
        turned.astype(BF16),
        patch_weight[0],
        vision_norm_gain,
        merger_weight[0],
        norm_gain,
        kv_weight[0],
        queries[0, 0],
        cotangent[0, 0],
        member_mask,
    )
    direction = direction.reshape(4, slot, pixels).transpose(1, 0, 2).reshape(images.shape)
    adversarial = jnp.clip(images + step_size[:, None, None] * direction, 0.0, 1.0)
    return adversarial, direction


def solution(mesh):
    placed = (
        P("dp", "tensor", None),
        P("dp"),
        P("group", "dp"),
        P("group", None, None),
        P("group", None),
        P("group", "dp", "tensor"),
        P("group", None),
        P("group", None, "dp", "tensor"),
        P("group", "dp", None, "tensor"),
        P("group", "dp", None, "tensor"),
    )
    return jax.shard_map(
        functools.partial(body, ng=mesh.shape["group"]),
        mesh=mesh,
        in_specs=placed,
        out_specs=(P("dp", "tensor", None), P("dp", "tensor", None)),
        check_vma=False,
    )
```

```python
import functools
import math

import jax
import jax.numpy as jnp
from jax import lax
from jax.experimental import pallas as pl
from jax.experimental.pallas import tpu as pltpu
from jax.sharding import PartitionSpec as P

F32 = jnp.float32
BF16 = jnp.bfloat16
NZ = 8
NT = 8
NY = 4
L = 128
AHEAD = 3
STOPS = (3, 5, 7, 8)
MESH = pl.DeviceIdType.MESH


def dot(a, b):
    return jnp.dot(a, b, preferred_element_type=F32)


def dot_nt(a, b):
    return lax.dot_general(a, b, (((1,), (1,)), ((), ())), preferred_element_type=F32)


def kernel(
    ng,
    n_pixels,
    pix_hbm,
    patch_hbm,
    vgain,
    w_ref,
    gain_ref,
    kv_ref,
    q_ref,
    cot_ref,
    mask_ref,
    step_ref,
    adv_hbm,
    dir_hbm,
    wg,
    kvl,
    tok,
    hid,
    part1,
    s1,
    r1,
    ssq_s,
    ssq_r,
    kvpre,
    kvt,
    kvh,
    gkvh,
    gkv,
    scal,
    part4,
    s4,
    r4,
    xhat,
    gbuf,
    sqb,
    patch_w,
    heads_in,
    pix,
    adv_ref,
    dir_ref,
    local_sem,
    zs,
    zr,
    xs,
    xr,
    as_,
    ar,
    rs1s,
    rs1r,
    sqs,
    sqr,
    ats,
    atr,
    bts,
    btr,
    ags,
    agr,
    scs,
    scr,
    rs4s,
    rs4r,
    grs,
    grr,
    fs,
    fr,
):
    g = lax.axis_index("group")
    d = lax.axis_index("dp")
    t = lax.axis_index("tensor")
    x, y = t // NY, lax.rem(t, NY)
    rows = w_ref.shape[0]
    slot = tok.shape[2]
    ntok = NZ * slot

    def zmod(i):
        return lax.rem(i + 2 * NZ, NZ)

    def cols(i):
        return pl.ds(pl.multiple_of(i * L, L), L)

    def remote(src, dst, send, recv, **to):
        return pltpu.make_async_remote_copy(
            src_ref=src, dst_ref=dst, send_sem=send, recv_sem=recv, device_id=to, device_id_type=MESH
        )

    sent = []

    def start(copy):
        copy.start()
        sent.append(copy)

    load_patch = pltpu.make_async_copy(patch_hbm, patch_w, local_sem.at[3])
    load_patch.start()
    load_pixels = pltpu.make_async_copy(pix_hbm.at[:, 0, :], pix, local_sem.at[4])
    load_pixels.start()
    barrier = pltpu.get_barrier_semaphore()
    for r in range(1, NZ):
        pl.semaphore_signal(barrier, inc=1, device_id={"dp": zmod(d + r)}, device_id_type=MESH)
    for r in range(1, NT):
        pl.semaphore_signal(barrier, inc=1, device_id={"tensor": lax.rem(t + r, NT)}, device_id_type=MESH)
    for r in range(1, ng):
        pl.semaphore_signal(barrier, inc=1, device_id={"group": lax.rem(g + r, ng)}, device_id_type=MESH)

    own = [pltpu.make_async_copy(w_ref.at[:, cols(d)], wg.at[d, :, cols(t)], local_sem.at[0])]
    for k in range(2):
        own.append(
            pltpu.make_async_copy(kv_ref.at[k, cols(d), :], kvl.at[k, cols(d), cols(t)], local_sem.at[1 + k])
        )
    for c in own:
        c.start()
    pl.semaphore_wait(barrier, NZ - 1 + NT - 1 + ng - 1)

    up = x * NY + lax.rem(y + 1, NY)
    down = x * NY + lax.rem(y + NY - 1, NY)
    far = x * NY + lax.rem(y + 2, NY)
    xo = (1 - x) * NY
    across = xo + y
    def kinds(height):
        part = height // 6 // 16 * 16
        whole, lo, hi = (0, height), (0, height // 2), (height // 2, height // 2)
        first, rest = (0, part), (part, height - part)
        return (
            (t, up, down, whole),
            (t, down, up, whole),
            (t, across, across, whole),
            (down, up, far, lo),
            (up, down, far, hi),
            (across, up, xo + lax.rem(y + NY - 1, NY), rest),
            (across, down, xo + lax.rem(y + 1, NY), rest),
            (far, across, xo + lax.rem(y + 2, NY), whole),
            (up, across, xo + lax.rem(y + 1, NY), first),
            (down, across, xo + lax.rem(y + NY - 1, NY), first),
        )

    def plane(p):
        step = (p + 1) // 2
        return zmod(d + jnp.where(lax.rem(p, 2) == 1, step, -step))

    def is_kv(p):
        return isinstance(p, int) and p >= NZ

    def xy(kind, p, incoming=False):
        buf = kvl.at[p - NZ] if is_kv(p) else wg.at[plane(jnp.int32(p))]
        block, to, arrives, (at, size) = kinds(buf.shape[0])[kind]
        view = buf.at[pl.ds(at, size), cols(arrives if incoming else block)]
        src = w_ref.at[:, cols(d)] if isinstance(p, int) and p == 0 and kind < 3 and not incoming else view
        return remote(src, view, xs.at[kind, p], xr.at[kind, p], tensor=to)

    def z_copy(p, which, incoming=False):
        step = (p + 1) // 2
        j = zmod(d + jnp.where(lax.rem(p, 2) == 1, -step, step))
        home = plane(p) if incoming else d
        if which == 0:
            src, dst = w_ref.at[:, cols(j)], wg.at[home, :, cols(t)]
        else:
            src, dst = kv_ref.at[which - 1, cols(j), :], kvl.at[which - 1, cols(home), cols(t)]
        return remote(src, dst, zs.at[which, p], zr.at[which, p], dp=j)

    def stage_a(p):
        if is_kv(p):
            for other in range(1, NZ):
                z_copy(jnp.int32(other), p - NZ + 1, True).wait_recv()
        else:
            z_copy(p, 0, True).wait_recv()
        for kind in (0, 1, 2):
            xy(kind, p).start()

    def stage_b(p):
        xy(0, p, True).wait_recv()
        xy(3, p).start()
        xy(9, p).start()
        xy(1, p, True).wait_recv()
        xy(4, p).start()
        xy(8, p).start()
        xy(2, p, True).wait_recv()
        xy(5, p).start()
        xy(6, p).start()

    def stage_c(p):
        xy(3, p, True).wait_recv()
        xy(4, p, True).wait_recv()
        xy(7, p).start()

    def stage_d(p):
        for kind in (5, 6, 7, 8, 9):
            xy(kind, p, True).wait_recv()

    for kind in (0, 1, 2):
        xy(kind, 0).start()
    for p in range(1, AHEAD + 1):
        z_copy(jnp.int32(p), 0).start()

    patches = pix.shape[1]
    natural = lax.broadcasted_iota(jnp.int32, (patches, patches), 0)
    turned = lax.broadcasted_iota(jnp.int32, (patches, patches), 1)
    per = patches // slot
    swap = jnp.where(turned == lax.rem(natural, per) * slot + natural // per, 1.0, 0.0).astype(BF16)
    back = jnp.where(natural == lax.rem(turned, per) * slot + turned // per, 1.0, 0.0).astype(BF16)
    load_pixels.wait()
    pixels = dot_nt(back, pix[...].astype(BF16)).astype(BF16)
    load_patch.wait()
    embed = dot(pixels, patch_w[...])
    centered = embed - jnp.mean(embed, -1, keepdims=True)
    inv_dev = lax.rsqrt(jnp.mean(centered * centered, -1, keepdims=True) + 1e-06)
    normalized = centered * inv_dev
    xhat[...] = normalized
    visual = (normalized * vgain[...]).astype(BF16)
    for s in range(NZ):
        j, h = s // 2, s % 2
        tok[d, s] = visual[j * slot : (j + 1) * slot, h * rows : (h + 1) * rows]

    def ring_gather(buf, send, recv, views):
        n = len(views)

        def copy(src, k, side, c):
            view = buf.at[(src,) + views[c]]
            to = zmod(d + 1 - 2 * side)
            return remote(view, view, send.at[side, k - 1, c], recv.at[side, k - 1, c], dp=to)

        def order(k, side):
            own_half = list(range(side * n // 2, (side + 1) * n // 2))
            return own_half if k == NZ // 2 else own_half + [c for c in range(n) if c not in own_half]

        def go(k):
            for i in range(n):
                for side in (0, 1):
                    if i < len(order(k, side)):
                        start(copy(zmod(d - (1 - 2 * side) * (k - 1)), k, side, order(k, side)[i]))

        def arrive(k, then_go=False):
            for i in range(n):
                for side in (0, 1):
                    if i < len(order(k, side)):
                        src, c = zmod(d - (1 - 2 * side) * k), order(k, side)[i]
                        copy(src, k, side, c).wait_recv()
                        if then_go and c in order(k + 1, side):
                            start(copy(src, k + 1, side, c))

        return go, arrive

    go, arrive = ring_gather(tok, as_, ar, [(pl.ds(0, NZ // 2),), (pl.ds(NZ // 2, NZ // 2),)])
    go(1)
    heads = q_ref.shape[1] // L
    heads_in[0] = jnp.concatenate([q_ref[:, h * L : (h + 1) * L] for h in range(heads)], axis=0)
    masked = (cot_ref[...].astype(F32) * mask_ref[...].astype(F32)).astype(BF16)
    heads_in[1] = jnp.concatenate([masked[:, h * L : (h + 1) * L] for h in range(heads)], axis=0)
    hid[...] = jnp.zeros_like(hid)
    for c in own:
        c.wait()

    def piece(p, carry):
        s = plane(p)
        hid[...] += dot(tok[:, s].reshape(ntok, rows), wg[s])
        return carry

    def pieces(start_at, stop_at):
        lax.fori_loop(start_at, stop_at, piece, 0)

    def weights_step(i, carry):
        stage_a(i)

        @pl.when(i + AHEAD < NZ)
        def _():
            z_copy(i + AHEAD, 0).start()

        stage_b(i - 1)

        @pl.when(i >= 2)
        def _():
            stage_c(i - 2)

        @pl.when(i >= 3)
        def _():
            stage_d(i - 3)

        return carry

    at = 1
    for k, stop in enumerate(STOPS):
        lax.fori_loop(at, stop, weights_step, 0)
        arrive(k + 1, k < 3)
        if k in (1, 2):
            for p in range(1, NZ):
                start(z_copy(jnp.int32(p), k))
        at = stop
    stage_a(NZ)
    stage_b(NZ - 1)
    stage_c(NZ - 2)
    pieces(0, 3)
    stage_d(NZ - 3)
    stage_a(NZ + 1)
    stage_b(NZ)
    stage_c(NZ - 1)
    pieces(3, 6)
    stage_d(NZ - 2)
    stage_b(NZ + 1)
    stage_c(NZ)
    pieces(6, 7)
    stage_d(NZ - 1)
    pieces(7, NZ)
    stage_c(NZ + 1)

    hidden = hid[...].astype(BF16).astype(F32)
    hid[...] = hidden
    gain = jnp.concatenate(
        [gain_ref[:, pl.ds(pl.multiple_of((b * NZ + d) * L, L), L)] for b in range(NT)], axis=-1
    )
    total_sq = jnp.sum(hidden * hidden, -1, keepdims=True)
    ssq_s[...] = jnp.broadcast_to(total_sq, (ntok, L)).reshape(NZ, slot, L)
    for r in range(1, NZ):
        j = zmod(d + r)
        start(remote(ssq_s.at[j], ssq_r.at[d], sqs.at[r], sqr.at[r], dp=j))
    ssq_r[d] = ssq_s[d]
    scaled = (hidden * gain).astype(BF16)
    def ring_sum(part, sbuf, rbuf, send, recv, chunks, n):
        def copy(k, c, side):
            sign = 1 - 2 * side
            if k == 1:
                at = pl.ds((2 * c + side) * n, n)
            else:
                at = pl.ds(2 * c * n, 2 * n)
            return remote(
                sbuf.at[side, k - 1, at],
                rbuf.at[side, k - 1, at],
                send.at[side, k - 1, c],
                recv.at[side, k - 1, c],
                dp=zmod(d + sign),
            )

        def step(k, c):
            for side in (0, 1):
                sign = 1 - 2 * side
                e = zmod(d + sign * (NZ // 2 + 1 - k))
                if k > 1:
                    copy(k - 1, c, side).wait_recv()
                for b in range(2):
                    at = pl.ds((2 * c + b) * n, n)
                    if k == 1 and b != side:
                        continue
                    value = part[e, at]
                    if k > 2 or (k == 2 and b == side):
                        value = value + rbuf[side, k - 2, at].astype(F32)
                    sbuf[side, k - 1, at] = value.astype(BF16)
                start(copy(k, c, side))

        def result(c):
            at = pl.ds(2 * c * n, 2 * n)
            value = part[d, at]
            for side in (0, 1):
                copy(NZ // 2, c, side).wait_recv()
                value = value + rbuf[side, NZ // 2 - 1, at].astype(F32)
            return value

        return step, result

    chunks = NZ // 2
    step, result = ring_sum(part1, s1, r1, rs1s, rs1r, chunks, 1)
    for k in range(2):
        stage_d(NZ + k)
        mine = (2 * k, 2 * k + 1)
        for c in mine:
            at = c % 2 * 4 * L
            share = dot(scaled, kvl[k, :, at : at + 4 * L])
            for b in range(2):
                part1[:, 2 * c + b] = share[:, 2 * b * L : 2 * (b + 1) * L].reshape(NZ, slot, 2 * L)
            step(1, c)
    for i in range(2, NZ // 2 + 1):
        for c in range(chunks):
            step(i, c)
    for r in range(1, NZ):
        j = zmod(d - r)
        remote(ssq_s.at[j], ssq_r.at[j], sqs.at[r], sqr.at[r], dp=j).wait_recv()
    width = gain_ref.shape[1]
    root = lax.rsqrt(jnp.sum(ssq_r[...], axis=0) / width + 1e-06)[:, :1]
    for c in range(chunks):
        pre = result(c)
        for b in range(2):
            at = (c % 2 * 2 + b) * 2 * L
            kvpre[c // 2, :, at : at + 2 * L] = pre[b]
            kvt[c // 2, :, at : at + 2 * L] = (pre[b] * root).astype(BF16)

    for r in range(1, NT):
        j = lax.rem(t + r, NT)
        start(remote(kvt.at[:, :, cols(j)], kvh.at[t], ats.at[r], atr.at[r], tensor=j))
    kvh[t] = kvt[:, :, cols(t)]
    query, grad_out = heads_in[0], heads_in[1]
    for r in range(1, NT):
        j = lax.rem(t + NT - r, NT)
        remote(kvh.at[j], kvh.at[j], ats.at[r], atr.at[r], tensor=j).wait_recv()
    scale = 1.0 / math.sqrt(L)
    keys = kvh[:, 0].reshape(ntok, L)
    values = kvh[:, 1].reshape(ntok, L)
    scores = dot_nt(keys, query) * scale
    e = jnp.exp(scores - jnp.max(scores, axis=0, keepdims=True))
    probs = e / jnp.sum(e, axis=0, keepdims=True)
    grad_probs = dot_nt(values, grad_out)
    inner = jnp.sum(probs * grad_probs, axis=0, keepdims=True)
    grad_scores = (probs * (grad_probs - inner) * scale).astype(BF16)
    gkvh[:, 0] = dot(grad_scores, query).astype(BF16).reshape(NT, slot, L)
    gkvh[:, 1] = dot(probs.astype(BF16), grad_out).astype(BF16).reshape(NT, slot, L)
    for r in range(1, NT):
        j = lax.rem(t + r, NT)
        start(remote(gkvh.at[j], gkv.at[d, :, :, cols(t)], bts.at[r], btr.at[r], tensor=j))
    gkv[d, :, :, cols(t)] = gkvh[t]
    for r in range(1, NT):
        j = lax.rem(t + NT - r, NT)
        remote(gkvh.at[j], gkv.at[d, :, :, cols(j)], bts.at[r], btr.at[r], tensor=j).wait_recv()

    spans = [(k, slice(None), pl.ds(h * 4 * L, 4 * L)) for k in range(2) for h in range(2)]
    go, arrive = ring_gather(gkv, ags, agr, spans)
    go(1)
    products = gkv[d].astype(F32) * kvpre[...]
    row_sum = jnp.sum(products[0] + products[1], -1, keepdims=True)
    coef = root * root * root * row_sum / width
    lane = lax.broadcasted_iota(jnp.int32, (slot, L), 1)
    scal[d] = jnp.where(lane < L // 2, root, coef)
    for r in range(1, NZ):
        start(remote(scal.at[d], scal.at[d], scs.at[r], scr.at[r], dp=zmod(d + r)))
    for k in range(1, NZ // 2):
        arrive(k, True)
    arrive(NZ // 2)
    for r in range(1, NZ):
        j = zmod(d - r)
        remote(scal.at[j], scal.at[j], scs.at[r], scr.at[r], dp=j).wait_recv()
    grad_feat = dot_nt(gkv[:, 0].reshape(ntok, NT * L), kvl[0]) + dot_nt(
        gkv[:, 1].reshape(ntok, NT * L), kvl[1]
    )
    both = scal[...].reshape(ntok, L)
    grad_hidden = (both[:, :1] * gain * grad_feat - hid[...] * both[:, L - 1 :]).astype(BF16)

    step, result = ring_sum(part4, s4, r4, rs4s, rs4r, chunks, 1)
    for c in range(chunks):
        for b in range(2):
            s = 2 * c + b
            part4[:, s] = dot_nt(grad_hidden, wg[s]).reshape(NZ, slot, rows)
        step(1, c)
    for k in range(2, NZ // 2 + 1):
        for c in range(chunks):
            step(k, c)
    blocks = []
    for c in range(chunks):
        value = result(c)
        blocks.append(jnp.concatenate([value[0], value[1]], axis=-1))
    grad_visual = jnp.concatenate(blocks, axis=0)

    gain_grad = grad_visual * vgain[...]
    normalized = xhat[...]
    embed_grad = (
        inv_dev
        * (
            gain_grad
            - jnp.mean(gain_grad, -1, keepdims=True)
            - normalized * jnp.mean(gain_grad * normalized, -1, keepdims=True)
        )
    ).astype(BF16)
    embed_grad = dot(swap, embed_grad).astype(BF16)
    gbuf[g] = dot_nt(patch_w[...], embed_grad).astype(BF16)
    for r in range(1, ng):
        start(remote(gbuf.at[g], gbuf.at[g], grs.at[r], grr.at[r], group=lax.rem(g + r, ng)))
    for r in range(1, ng):
        j = lax.rem(g + ng - r, ng)
        remote(gbuf.at[j], gbuf.at[j], grs.at[r], grr.at[r], group=j).wait_recv()
    gradient = gbuf[0].astype(F32)
    for m in range(1, ng):
        gradient = gradient + gbuf[m].astype(F32)
    sqb[t] = jnp.broadcast_to(jnp.sum(gradient * gradient), (8, L))
    for r in range(1, NT):
        start(remote(sqb.at[t], sqb.at[t], fs.at[r], fr.at[r], tensor=lax.rem(t + r, NT)))
    for r in range(1, NT):
        j = lax.rem(t + NT - r, NT)
        remote(sqb.at[j], sqb.at[j], fs.at[r], fr.at[r], tensor=j).wait_recv()
    squares = jnp.sum(sqb[...], axis=0)[:1, :1]
    direction = jnp.tanh(gradient * lax.rsqrt(squares / n_pixels + 1e-06))
    dir_ref[...] = direction
    stores = [pltpu.make_async_copy(dir_ref, dir_hbm.at[:, 0, :], local_sem.at[5])]
    stores[0].start()
    adv_ref[...] = jnp.clip(pix[...] + step_ref[...] * direction, 0.0, 1.0)
    stores.append(pltpu.make_async_copy(adv_ref, adv_hbm.at[:, 0, :], local_sem.at[6]))
    stores[1].start()
    for c in stores:
        c.wait()

    for copy in sent:
        copy.wait_send()

    def drain(p, carry):
        for kind in range(10):
            xy(kind, p).wait_send()

        @pl.when(p > 0)
        def _():
            z_copy(p, 0).wait_send()

        return carry

    lax.fori_loop(0, NZ, drain, 0)
    for p in (NZ, NZ + 1):
        for kind in range(10):
            xy(kind, p).wait_send()


def body(
    images,
    step_size,
    member_mask,
    patch_weight,
    vision_norm_gain,
    merger_weight,
    norm_gain,
    kv_weight,
    queries,
    cotangent,
    *,
    ng,
):
    patches, pixels = images.shape[1:]
    slot = patches // 4
    rows, width = merger_weight.shape[1:]
    vwidth = patch_weight.shape[2]
    half = NZ // 2
    dma = pltpu.SemaphoreType.DMA
    vmem = pl.BlockSpec(memory_space=pltpu.VMEM)
    anywhere = pl.BlockSpec(memory_space=pl.ANY)
    flipped = jax.ShapeDtypeStruct((pixels, 1, patches), F32)
    adversarial, direction = pl.pallas_call(
        functools.partial(kernel, ng, float(NT * patches * pixels)),
        out_shape=(flipped, flipped),
        in_specs=[anywhere, anywhere, vmem, anywhere, vmem, anywhere, vmem, vmem, vmem, vmem],
        out_specs=(anywhere, anywhere),
        scratch_shapes=[
            pltpu.VMEM((NZ, rows, NT * L), BF16),
            pltpu.VMEM((2, NZ * L, NT * L), BF16),
            pltpu.VMEM((NZ, NZ, slot, rows), BF16),
            pltpu.VMEM((NZ * slot, NT * L), F32),
            pltpu.VMEM((NZ, NZ, slot, 2 * L), F32),
            pltpu.VMEM((2, half, NZ, slot, 2 * L), BF16),
            pltpu.VMEM((2, half, NZ, slot, 2 * L), BF16),
            pltpu.VMEM((NZ, slot, L), F32),
            pltpu.VMEM((NZ, slot, L), F32),
            pltpu.VMEM((2, slot, NT * L), F32),
            pltpu.VMEM((2, slot, NT * L), BF16),
            pltpu.VMEM((NT, 2, slot, L), BF16),
            pltpu.VMEM((NT, 2, slot, L), BF16),
            pltpu.VMEM((NZ, 2, slot, NT * L), BF16),
            pltpu.VMEM((NZ, slot, L), F32),
            pltpu.VMEM((NZ, NZ, slot, rows), F32),
            pltpu.VMEM((2, half, NZ, slot, rows), BF16),
            pltpu.VMEM((2, half, NZ, slot, rows), BF16),
            pltpu.VMEM((patches, vwidth), F32),
            pltpu.VMEM((ng, pixels, patches), BF16),
            pltpu.VMEM((NT, 8, L), F32),
            pltpu.VMEM((pixels, vwidth), BF16),
            pltpu.VMEM((2, NZ * slot, L), BF16),
            pltpu.VMEM((pixels, patches), F32),
            pltpu.VMEM((pixels, patches), F32),
            pltpu.VMEM((pixels, patches), F32),
            dma((7,)),
            dma((3, NZ)),
            dma((3, NZ)),
            dma((10, NZ + 2)),
            dma((10, NZ + 2)),
            dma((2, half, 2)),
            dma((2, half, 2)),
            dma((2, half, half)),
            dma((2, half, half)),
            dma((NZ,)),
            dma((NZ,)),
            dma((NT,)),
            dma((NT,)),
            dma((NT,)),
            dma((NT,)),
            dma((2, half, half)),
            dma((2, half, half)),
            dma((NZ,)),
            dma((NZ,)),
            dma((2, half, half)),
            dma((2, half, half)),
            dma((max(ng, 2),)),
            dma((max(ng, 2),)),
            dma((NT,)),
            dma((NT,)),
        ],
        compiler_params=pltpu.CompilerParams(
            collective_id=0, has_side_effects=True, vmem_limit_bytes=60 * 1024 * 1024
        ),
    )(
        images.transpose(2, 0, 1),
        patch_weight[0],
        vision_norm_gain,
        merger_weight[0],
        norm_gain,
        kv_weight[0],
        queries[0, 0],
        cotangent[0, 0],
        member_mask,
        step_size[None],
    )
    return adversarial.transpose(1, 2, 0), direction.transpose(1, 2, 0)


def solution(mesh):
    placed = (
        P("dp", "tensor", None),
        P("dp"),
        P("group", "dp"),
        P("group", None, None),
        P("group", None),
        P("group", "dp", "tensor"),
        P("group", None),
        P("group", None, "dp", "tensor"),
        P("group", "dp", None, "tensor"),
        P("group", "dp", None, "tensor"),
    )
    return jax.shard_map(
        functools.partial(body, ng=mesh.shape["group"]),
        mesh=mesh,
        in_specs=placed,
        out_specs=(P("dp", "tensor", None), P("dp", "tensor", None)),
        check_vma=False,
    )
```

```python
import functools
import math

import jax
import jax.numpy as jnp
from jax import lax
from jax.experimental import pallas as pl
from jax.experimental.pallas import tpu as pltpu
from jax.sharding import PartitionSpec as P

F32 = jnp.float32
BF16 = jnp.bfloat16
NZ = 8
NT = 8
NY = 4
L = 128
AHEAD = 3
STOPS = (3, 5, 7, 8)
MESH = pl.DeviceIdType.MESH


def dot(a, b):
    return jnp.dot(a, b, preferred_element_type=F32)


def dot_nt(a, b):
    return lax.dot_general(a, b, (((1,), (1,)), ((), ())), preferred_element_type=F32)


def kernel(
    ng,
    n_pixels,
    pix_hbm,
    patch_hbm,
    vgain,
    w_ref,
    gain_ref,
    kv_ref,
    q_ref,
    cot_ref,
    mask_ref,
    dir_hbm,
    wg,
    kvl,
    tok,
    hid,
    part1,
    s1,
    r1,
    ssq_s,
    ssq_r,
    kvpre,
    kvt,
    kvh,
    gkvh,
    gkv,
    scal,
    part4,
    s4,
    r4,
    xhat,
    gbuf,
    sqb,
    patch_w,
    heads_in,
    pix,
    dir_ref,
    local_sem,
    zs,
    zr,
    xs,
    xr,
    as_,
    ar,
    rs1s,
    rs1r,
    sqs,
    sqr,
    ats,
    atr,
    bts,
    btr,
    ags,
    agr,
    scs,
    scr,
    rs4s,
    rs4r,
    grs,
    grr,
    fs,
    fr,
):
    g = lax.axis_index("group")
    d = lax.axis_index("dp")
    t = lax.axis_index("tensor")
    x, y = t // NY, lax.rem(t, NY)
    rows = w_ref.shape[0]
    slot = tok.shape[2]
    ntok = NZ * slot

    def zmod(i):
        return lax.rem(i + 2 * NZ, NZ)

    def cols(i):
        return pl.ds(pl.multiple_of(i * L, L), L)

    def remote(src, dst, send, recv, **to):
        return pltpu.make_async_remote_copy(
            src_ref=src, dst_ref=dst, send_sem=send, recv_sem=recv, device_id=to, device_id_type=MESH
        )

    sent = []

    def start(copy):
        copy.start()
        sent.append(copy)

    load_patch = pltpu.make_async_copy(patch_hbm, patch_w, local_sem.at[3])
    load_patch.start()
    load_pixels = pltpu.make_async_copy(pix_hbm.at[:, 0, :], pix, local_sem.at[4])
    load_pixels.start()
    barrier = pltpu.get_barrier_semaphore()
    for r in range(1, NZ):
        pl.semaphore_signal(barrier, inc=1, device_id={"dp": zmod(d + r)}, device_id_type=MESH)
    for r in range(1, NT):
        pl.semaphore_signal(barrier, inc=1, device_id={"tensor": lax.rem(t + r, NT)}, device_id_type=MESH)
    for r in range(1, ng):
        pl.semaphore_signal(barrier, inc=1, device_id={"group": lax.rem(g + r, ng)}, device_id_type=MESH)

    own = [pltpu.make_async_copy(w_ref.at[:, cols(d)], wg.at[d, :, cols(t)], local_sem.at[0])]
    for k in range(2):
        own.append(
            pltpu.make_async_copy(kv_ref.at[k, cols(d), :], kvl.at[k, cols(d), cols(t)], local_sem.at[1 + k])
        )
    for c in own:
        c.start()
    pl.semaphore_wait(barrier, NZ - 1 + NT - 1 + ng - 1)

    up = x * NY + lax.rem(y + 1, NY)
    down = x * NY + lax.rem(y + NY - 1, NY)
    far = x * NY + lax.rem(y + 2, NY)
    xo = (1 - x) * NY
    across = xo + y
    def kinds(height):
        part = height // 6 // 16 * 16
        whole, lo, hi = (0, height), (0, height // 2), (height // 2, height // 2)
        first, rest = (0, part), (part, height - part)
        return (
            (t, up, down, whole),
            (t, down, up, whole),
            (t, across, across, whole),
            (down, up, far, lo),
            (up, down, far, hi),
            (across, up, xo + lax.rem(y + NY - 1, NY), rest),
            (across, down, xo + lax.rem(y + 1, NY), rest),
            (far, across, xo + lax.rem(y + 2, NY), whole),
            (up, across, xo + lax.rem(y + 1, NY), first),
            (down, across, xo + lax.rem(y + NY - 1, NY), first),
        )

    def plane(p):
        step = (p + 1) // 2
        return zmod(d + jnp.where(lax.rem(p, 2) == 1, step, -step))

    def is_kv(p):
        return isinstance(p, int) and p >= NZ

    def xy(kind, p, incoming=False):
        buf = kvl.at[p - NZ] if is_kv(p) else wg.at[plane(jnp.int32(p))]
        block, to, arrives, (at, size) = kinds(buf.shape[0])[kind]
        view = buf.at[pl.ds(at, size), cols(arrives if incoming else block)]
        src = w_ref.at[:, cols(d)] if isinstance(p, int) and p == 0 and kind < 3 and not incoming else view
        return remote(src, view, xs.at[kind, p], xr.at[kind, p], tensor=to)

    def z_copy(p, which, incoming=False):
        step = (p + 1) // 2
        j = zmod(d + jnp.where(lax.rem(p, 2) == 1, -step, step))
        home = plane(p) if incoming else d
        if which == 0:
            src, dst = w_ref.at[:, cols(j)], wg.at[home, :, cols(t)]
        else:
            src, dst = kv_ref.at[which - 1, cols(j), :], kvl.at[which - 1, cols(home), cols(t)]
        return remote(src, dst, zs.at[which, p], zr.at[which, p], dp=j)

    def stage_a(p):
        if is_kv(p):
            for other in range(1, NZ):
                z_copy(jnp.int32(other), p - NZ + 1, True).wait_recv()
        else:
            z_copy(p, 0, True).wait_recv()
        for kind in (0, 1, 2):
            xy(kind, p).start()

    def stage_b(p):
        xy(0, p, True).wait_recv()
        xy(3, p).start()
        xy(9, p).start()
        xy(1, p, True).wait_recv()
        xy(4, p).start()
        xy(8, p).start()
        xy(2, p, True).wait_recv()
        xy(5, p).start()
        xy(6, p).start()

    def stage_c(p):
        xy(3, p, True).wait_recv()
        xy(4, p, True).wait_recv()
        xy(7, p).start()

    def stage_d(p):
        for kind in (5, 6, 7, 8, 9):
            xy(kind, p, True).wait_recv()

    for kind in (0, 1, 2):
        xy(kind, 0).start()
    for p in range(1, AHEAD + 1):
        z_copy(jnp.int32(p), 0).start()

    patches = pix.shape[1]
    natural = lax.broadcasted_iota(jnp.int32, (patches, patches), 0)
    turned = lax.broadcasted_iota(jnp.int32, (patches, patches), 1)
    per = patches // slot
    back = jnp.where(natural == lax.rem(turned, per) * slot + turned // per, 1.0, 0.0).astype(BF16)
    load_pixels.wait()
    pixels = dot_nt(back, pix[...].astype(BF16)).astype(BF16)
    load_patch.wait()
    embed = dot(pixels, patch_w[...])
    centered = embed - jnp.mean(embed, -1, keepdims=True)
    inv_dev = lax.rsqrt(jnp.mean(centered * centered, -1, keepdims=True) + 1e-06)
    normalized = centered * inv_dev
    xhat[...] = normalized
    visual = (normalized * vgain[...]).astype(BF16)
    for s in range(NZ):
        j, h = s // 2, s % 2
        tok[d, s] = visual[j * slot : (j + 1) * slot, h * rows : (h + 1) * rows]

    def ring_gather(buf, send, recv, views):
        n = len(views)

        def copy(src, k, side, c):
            view = buf.at[(src,) + views[c]]
            to = zmod(d + 1 - 2 * side)
            return remote(view, view, send.at[side, k - 1, c], recv.at[side, k - 1, c], dp=to)

        def order(k, side):
            own_half = list(range(side * n // 2, (side + 1) * n // 2))
            return own_half if k == NZ // 2 else own_half + [c for c in range(n) if c not in own_half]

        def go(k):
            for i in range(n):
                for side in (0, 1):
                    if i < len(order(k, side)):
                        start(copy(zmod(d - (1 - 2 * side) * (k - 1)), k, side, order(k, side)[i]))

        def arrive(k, then_go=False):
            for i in range(n):
                for side in (0, 1):
                    if i < len(order(k, side)):
                        src, c = zmod(d - (1 - 2 * side) * k), order(k, side)[i]
                        copy(src, k, side, c).wait_recv()
                        if then_go and c in order(k + 1, side):
                            start(copy(src, k + 1, side, c))

        return go, arrive

    go, arrive = ring_gather(tok, as_, ar, [(pl.ds(0, NZ // 2),), (pl.ds(NZ // 2, NZ // 2),)])
    go(1)
    heads = q_ref.shape[1] // L
    heads_in[0] = jnp.concatenate([q_ref[:, h * L : (h + 1) * L] for h in range(heads)], axis=0)
    masked = (cot_ref[...].astype(F32) * mask_ref[...].astype(F32)).astype(BF16)
    heads_in[1] = jnp.concatenate([masked[:, h * L : (h + 1) * L] for h in range(heads)], axis=0)
    hid[...] = jnp.zeros_like(hid)
    for c in own:
        c.wait()

    def piece(p, carry):
        s = plane(p)
        hid[...] += dot(tok[:, s].reshape(ntok, rows), wg[s])
        return carry

    def pieces(start_at, stop_at):
        lax.fori_loop(start_at, stop_at, piece, 0)

    def weights_step(i, carry):
        stage_a(i)

        @pl.when(i + AHEAD < NZ)
        def _():
            z_copy(i + AHEAD, 0).start()

        stage_b(i - 1)

        @pl.when(i >= 2)
        def _():
            stage_c(i - 2)

        @pl.when(i >= 3)
        def _():
            stage_d(i - 3)

        return carry

    at = 1
    for k, stop in enumerate(STOPS):
        lax.fori_loop(at, stop, weights_step, 0)
        arrive(k + 1, k < 3)
        if k in (1, 2):
            for p in range(1, NZ):
                start(z_copy(jnp.int32(p), k))
        at = stop
    stage_a(NZ)
    stage_b(NZ - 1)
    stage_c(NZ - 2)
    pieces(0, 3)
    stage_d(NZ - 3)
    stage_a(NZ + 1)
    stage_b(NZ)
    stage_c(NZ - 1)
    pieces(3, 6)
    stage_d(NZ - 2)
    stage_b(NZ + 1)
    stage_c(NZ)
    pieces(6, 7)
    stage_d(NZ - 1)
    pieces(7, NZ)
    stage_c(NZ + 1)

    hidden = hid[...].astype(BF16).astype(F32)
    hid[...] = hidden
    gain = jnp.concatenate(
        [gain_ref[:, pl.ds(pl.multiple_of((b * NZ + d) * L, L), L)] for b in range(NT)], axis=-1
    )
    total_sq = jnp.sum(hidden * hidden, -1, keepdims=True)
    ssq_s[...] = jnp.broadcast_to(total_sq, (ntok, L)).reshape(NZ, slot, L)
    for r in range(1, NZ):
        j = zmod(d + r)
        start(remote(ssq_s.at[j], ssq_r.at[d], sqs.at[r], sqr.at[r], dp=j))
    ssq_r[d] = ssq_s[d]
    scaled = (hidden * gain).astype(BF16)
    def ring_sum(part, sbuf, rbuf, send, recv, chunks, n):
        def copy(k, c, side):
            sign = 1 - 2 * side
            if k == 1:
                at = pl.ds((2 * c + side) * n, n)
            else:
                at = pl.ds(2 * c * n, 2 * n)
            return remote(
                sbuf.at[side, k - 1, at],
                rbuf.at[side, k - 1, at],
                send.at[side, k - 1, c],
                recv.at[side, k - 1, c],
                dp=zmod(d + sign),
            )

        def step(k, c):
            for side in (0, 1):
                sign = 1 - 2 * side
                e = zmod(d + sign * (NZ // 2 + 1 - k))
                if k > 1:
                    copy(k - 1, c, side).wait_recv()
                for b in range(2):
                    at = pl.ds((2 * c + b) * n, n)
                    if k == 1 and b != side:
                        continue
                    value = part[e, at]
                    if k > 2 or (k == 2 and b == side):
                        value = value + rbuf[side, k - 2, at].astype(F32)
                    sbuf[side, k - 1, at] = value.astype(BF16)
                start(copy(k, c, side))

        def result(c):
            at = pl.ds(2 * c * n, 2 * n)
            value = part[d, at]
            for side in (0, 1):
                copy(NZ // 2, c, side).wait_recv()
                value = value + rbuf[side, NZ // 2 - 1, at].astype(F32)
            return value

        return step, result

    chunks = NZ // 2
    step, result = ring_sum(part1, s1, r1, rs1s, rs1r, chunks, 1)
    for k in range(2):
        stage_d(NZ + k)
        mine = (2 * k, 2 * k + 1)
        for c in mine:
            at = c % 2 * 4 * L
            share = dot(scaled, kvl[k, :, at : at + 4 * L])
            for b in range(2):
                part1[:, 2 * c + b] = share[:, 2 * b * L : 2 * (b + 1) * L].reshape(NZ, slot, 2 * L)
            step(1, c)
    for i in range(2, NZ // 2 + 1):
        for c in range(chunks):
            step(i, c)
    for r in range(1, NZ):
        j = zmod(d - r)
        remote(ssq_s.at[j], ssq_r.at[j], sqs.at[r], sqr.at[r], dp=j).wait_recv()
    width = gain_ref.shape[1]
    root = lax.rsqrt(jnp.sum(ssq_r[...], axis=0) / width + 1e-06)[:, :1]
    for c in range(chunks):
        pre = result(c)
        for b in range(2):
            at = (c % 2 * 2 + b) * 2 * L
            kvpre[c // 2, :, at : at + 2 * L] = pre[b]
            kvt[c // 2, :, at : at + 2 * L] = (pre[b] * root).astype(BF16)

    for r in range(1, NT):
        j = lax.rem(t + r, NT)
        start(remote(kvt.at[:, :, cols(j)], kvh.at[t], ats.at[r], atr.at[r], tensor=j))
    kvh[t] = kvt[:, :, cols(t)]
    query, grad_out = heads_in[0], heads_in[1]
    for r in range(1, NT):
        j = lax.rem(t + NT - r, NT)
        remote(kvh.at[j], kvh.at[j], ats.at[r], atr.at[r], tensor=j).wait_recv()
    scale = 1.0 / math.sqrt(L)
    keys = kvh[:, 0].reshape(ntok, L)
    values = kvh[:, 1].reshape(ntok, L)
    scores = dot_nt(keys, query) * scale
    e = jnp.exp(scores - jnp.max(scores, axis=0, keepdims=True))
    probs = e / jnp.sum(e, axis=0, keepdims=True)
    grad_probs = dot_nt(values, grad_out)
    inner = jnp.sum(probs * grad_probs, axis=0, keepdims=True)
    grad_scores = (probs * (grad_probs - inner) * scale).astype(BF16)
    gkvh[:, 0] = dot(grad_scores, query).astype(BF16).reshape(NT, slot, L)
    gkvh[:, 1] = dot(probs.astype(BF16), grad_out).astype(BF16).reshape(NT, slot, L)
    for r in range(1, NT):
        j = lax.rem(t + r, NT)
        start(remote(gkvh.at[j], gkv.at[d, :, :, cols(t)], bts.at[r], btr.at[r], tensor=j))
    gkv[d, :, :, cols(t)] = gkvh[t]
    for r in range(1, NT):
        j = lax.rem(t + NT - r, NT)
        remote(gkvh.at[j], gkv.at[d, :, :, cols(j)], bts.at[r], btr.at[r], tensor=j).wait_recv()

    spans = [(k, slice(None), pl.ds(h * 4 * L, 4 * L)) for k in range(2) for h in range(2)]
    go, arrive = ring_gather(gkv, ags, agr, spans)
    go(1)
    products = gkv[d].astype(F32) * kvpre[...]
    row_sum = jnp.sum(products[0] + products[1], -1, keepdims=True)
    coef = root * root * root * row_sum / width
    lane = lax.broadcasted_iota(jnp.int32, (slot, L), 1)
    scal[d] = jnp.where(lane < L // 2, root, coef)
    for r in range(1, NZ):
        start(remote(scal.at[d], scal.at[d], scs.at[r], scr.at[r], dp=zmod(d + r)))
    for k in range(1, NZ // 2):
        arrive(k, True)
    arrive(NZ // 2)
    for r in range(1, NZ):
        j = zmod(d - r)
        remote(scal.at[j], scal.at[j], scs.at[r], scr.at[r], dp=j).wait_recv()
    grad_feat = dot_nt(gkv[:, 0].reshape(ntok, NT * L), kvl[0]) + dot_nt(
        gkv[:, 1].reshape(ntok, NT * L), kvl[1]
    )
    both = scal[...].reshape(ntok, L)
    grad_hidden = (both[:, :1] * gain * grad_feat - hid[...] * both[:, L - 1 :]).astype(BF16)

    step, result = ring_sum(part4, s4, r4, rs4s, rs4r, chunks, 1)
    for c in range(chunks):
        for b in range(2):
            s = 2 * c + b
            part4[:, s] = dot_nt(grad_hidden, wg[s]).reshape(NZ, slot, rows)
        step(1, c)
    for k in range(2, NZ // 2 + 1):
        for c in range(chunks):
            step(k, c)
    for c in range(chunks):
        value = result(c)
        gain_grad = jnp.concatenate([value[0], value[1]], axis=-1) * vgain[...]
        mine = pl.ds(c * slot, slot)
        normalized = xhat[mine, :]
        embed_grad = (
            inv_dev[c * slot : (c + 1) * slot]
            * (
                gain_grad
                - jnp.mean(gain_grad, -1, keepdims=True)
                - normalized * jnp.mean(gain_grad * normalized, -1, keepdims=True)
            )
        ).astype(BF16)
        gbuf[g, mine] = dot_nt(embed_grad, patch_w[...]).astype(BF16)
        for r in range(1, ng):
            view = gbuf.at[g, mine]
            start(remote(view, view, grs.at[r, c], grr.at[r, c], group=lax.rem(g + r, ng)))
    for c in range(chunks):
        for r in range(1, ng):
            j = lax.rem(g + ng - r, ng)
            view = gbuf.at[j, pl.ds(c * slot, slot)]
            remote(view, view, grs.at[r, c], grr.at[r, c], group=j).wait_recv()
    gradient = lax.dot_general(
        gbuf[...].reshape(ng * patches, -1),
        jnp.concatenate([back] * ng, axis=0),
        (((0,), (0,)), ((), ())),
        preferred_element_type=F32,
    )
    sqb[t] = jnp.broadcast_to(jnp.sum(gradient * gradient), (8, L))
    for r in range(1, NT):
        start(remote(sqb.at[t], sqb.at[t], fs.at[r], fr.at[r], tensor=lax.rem(t + r, NT)))
    for r in range(1, NT):
        j = lax.rem(t + NT - r, NT)
        remote(sqb.at[j], sqb.at[j], fs.at[r], fr.at[r], tensor=j).wait_recv()
    squares = jnp.sum(sqb[...], axis=0)[:1, :1]
    dir_ref[...] = gradient * lax.rsqrt(squares / n_pixels + 1e-06)
    store = pltpu.make_async_copy(dir_ref, dir_hbm.at[:, 0, :], local_sem.at[5])
    store.start()
    store.wait()

    for copy in sent:
        copy.wait_send()

    def drain(p, carry):
        for kind in range(10):
            xy(kind, p).wait_send()

        @pl.when(p > 0)
        def _():
            z_copy(p, 0).wait_send()

        return carry

    lax.fori_loop(0, NZ, drain, 0)
    for p in (NZ, NZ + 1):
        for kind in range(10):
            xy(kind, p).wait_send()


def body(
    images,
    step_size,
    member_mask,
    patch_weight,
    vision_norm_gain,
    merger_weight,
    norm_gain,
    kv_weight,
    queries,
    cotangent,
    *,
    ng,
):
    patches, pixels = images.shape[1:]
    slot = patches // 4
    rows, width = merger_weight.shape[1:]
    vwidth = patch_weight.shape[2]
    half = NZ // 2
    dma = pltpu.SemaphoreType.DMA
    vmem = pl.BlockSpec(memory_space=pltpu.VMEM)
    anywhere = pl.BlockSpec(memory_space=pl.ANY)
    normed = pl.pallas_call(
        functools.partial(kernel, ng, float(NT * patches * pixels)),
        out_shape=jax.ShapeDtypeStruct((pixels, 1, patches), F32),
        in_specs=[anywhere, anywhere, vmem, anywhere, vmem, anywhere, vmem, vmem, vmem],
        out_specs=anywhere,
        scratch_shapes=[
            pltpu.VMEM((NZ, rows, NT * L), BF16),
            pltpu.VMEM((2, NZ * L, NT * L), BF16),
            pltpu.VMEM((NZ, NZ, slot, rows), BF16),
            pltpu.VMEM((NZ * slot, NT * L), F32),
            pltpu.VMEM((NZ, NZ, slot, 2 * L), F32),
            pltpu.VMEM((2, half, NZ, slot, 2 * L), BF16),
            pltpu.VMEM((2, half, NZ, slot, 2 * L), BF16),
            pltpu.VMEM((NZ, slot, L), F32),
            pltpu.VMEM((NZ, slot, L), F32),
            pltpu.VMEM((2, slot, NT * L), F32),
            pltpu.VMEM((2, slot, NT * L), BF16),
            pltpu.VMEM((NT, 2, slot, L), BF16),
            pltpu.VMEM((NT, 2, slot, L), BF16),
            pltpu.VMEM((NZ, 2, slot, NT * L), BF16),
            pltpu.VMEM((NZ, slot, L), F32),
            pltpu.VMEM((NZ, NZ, slot, rows), F32),
            pltpu.VMEM((2, half, NZ, slot, rows), BF16),
            pltpu.VMEM((2, half, NZ, slot, rows), BF16),
            pltpu.VMEM((patches, vwidth), F32),
            pltpu.VMEM((ng, patches, pixels), BF16),
            pltpu.VMEM((NT, 8, L), F32),
            pltpu.VMEM((pixels, vwidth), BF16),
            pltpu.VMEM((2, NZ * slot, L), BF16),
            pltpu.VMEM((pixels, patches), F32),
            pltpu.VMEM((pixels, patches), F32),
            dma((6,)),
            dma((3, NZ)),
            dma((3, NZ)),
            dma((10, NZ + 2)),
            dma((10, NZ + 2)),
            dma((2, half, 2)),
            dma((2, half, 2)),
            dma((2, half, half)),
            dma((2, half, half)),
            dma((NZ,)),
            dma((NZ,)),
            dma((NT,)),
            dma((NT,)),
            dma((NT,)),
            dma((NT,)),
            dma((2, half, half)),
            dma((2, half, half)),
            dma((NZ,)),
            dma((NZ,)),
            dma((2, half, half)),
            dma((2, half, half)),
            dma((max(ng, 2), half)),
            dma((max(ng, 2), half)),
            dma((NT,)),
            dma((NT,)),
        ],
        compiler_params=pltpu.CompilerParams(
            collective_id=0, has_side_effects=True, vmem_limit_bytes=60 * 1024 * 1024
        ),
    )(
        images.transpose(2, 0, 1),
        patch_weight[0],
        vision_norm_gain,
        merger_weight[0],
        norm_gain,
        kv_weight[0],
        queries[0, 0],
        cotangent[0, 0],
        member_mask,
    )
    direction = jnp.tanh(normed.transpose(1, 2, 0))
    adversarial = jnp.clip(images + step_size[:, None, None] * direction, 0.0, 1.0)
    return adversarial, direction


def solution(mesh):
    placed = (
        P("dp", "tensor", None),
        P("dp"),
        P("group", "dp"),
        P("group", None, None),
        P("group", None),
        P("group", "dp", "tensor"),
        P("group", None),
        P("group", None, "dp", "tensor"),
        P("group", "dp", None, "tensor"),
        P("group", "dp", None, "tensor"),
    )
    return jax.shard_map(
        functools.partial(body, ng=mesh.shape["group"]),
        mesh=mesh,
        in_specs=placed,
        out_specs=(P("dp", "tensor", None), P("dp", "tensor", None)),
        check_vma=False,
    )
```

```python
import functools
import math

import jax
import jax.numpy as jnp
from jax import lax
from jax.experimental import pallas as pl
from jax.experimental.pallas import tpu as pltpu
from jax.sharding import PartitionSpec as P

F32 = jnp.float32
BF16 = jnp.bfloat16
NZ = 8
NT = 8
NY = 4
L = 128
AHEAD = 3
STOPS = (3, 5, 7, 8)
MESH = pl.DeviceIdType.MESH


def dot(a, b):
    return jnp.dot(a, b, preferred_element_type=F32)


def dot_nt(a, b):
    return lax.dot_general(a, b, (((1,), (1,)), ((), ())), preferred_element_type=F32)


def kernel(
    ng,
    n_pixels,
    pix_hbm,
    patch_hbm,
    vgain,
    w_ref,
    gain_ref,
    kv_ref,
    q_ref,
    cot_ref,
    mask_ref,
    dir_hbm,
    wg,
    kvl,
    tok,
    hid,
    part1,
    s1,
    r1,
    ssq_s,
    ssq_r,
    kvpre,
    kvt,
    kvh,
    gkvh,
    gkv,
    scal,
    part4,
    s4,
    r4,
    xhat,
    gbuf,
    sqb,
    patch_w,
    heads_in,
    pix,
    dir_ref,
    local_sem,
    zs,
    zr,
    xs,
    xr,
    as_,
    ar,
    rs1s,
    rs1r,
    sqs,
    sqr,
    ats,
    atr,
    bts,
    btr,
    ags,
    agr,
    scs,
    scr,
    rs4s,
    rs4r,
    grs,
    grr,
    fs,
    fr,
):
    g = lax.axis_index("group")
    d = lax.axis_index("dp")
    t = lax.axis_index("tensor")
    x, y = t // NY, lax.rem(t, NY)
    rows = w_ref.shape[0]
    slot = tok.shape[2]
    ntok = NZ * slot

    def zmod(i):
        return lax.rem(i + 2 * NZ, NZ)

    def cols(i):
        return pl.ds(pl.multiple_of(i * L, L), L)

    def remote(src, dst, send, recv, **to):
        return pltpu.make_async_remote_copy(
            src_ref=src, dst_ref=dst, send_sem=send, recv_sem=recv, device_id=to, device_id_type=MESH
        )

    sent = []

    def start(copy):
        copy.start()
        sent.append(copy)

    load_patch = pltpu.make_async_copy(patch_hbm, patch_w, local_sem.at[3])
    load_patch.start()
    load_pixels = pltpu.make_async_copy(pix_hbm.at[:, 0, :], pix, local_sem.at[4])
    load_pixels.start()
    barrier = pltpu.get_barrier_semaphore()
    for r in range(1, NZ):
        pl.semaphore_signal(barrier, inc=1, device_id={"dp": zmod(d + r)}, device_id_type=MESH)
    for r in range(1, NT):
        pl.semaphore_signal(barrier, inc=1, device_id={"tensor": lax.rem(t + r, NT)}, device_id_type=MESH)
    for r in range(1, ng):
        pl.semaphore_signal(barrier, inc=1, device_id={"group": lax.rem(g + r, ng)}, device_id_type=MESH)

    own = [pltpu.make_async_copy(w_ref.at[:, cols(d)], wg.at[d, :, cols(t)], local_sem.at[0])]
    for k in range(2):
        own.append(
            pltpu.make_async_copy(kv_ref.at[k, cols(d), :], kvl.at[k, cols(d), cols(t)], local_sem.at[1 + k])
        )
    for c in own:
        c.start()
    pl.semaphore_wait(barrier, NZ - 1 + NT - 1 + ng - 1)

    up = x * NY + lax.rem(y + 1, NY)
    down = x * NY + lax.rem(y + NY - 1, NY)
    far = x * NY + lax.rem(y + 2, NY)
    xo = (1 - x) * NY
    across = xo + y
    def kinds(height):
        part = height * 9 // 50 // 16 * 16
        whole, lo, hi = (0, height), (0, height // 2), (height // 2, height // 2)
        first, rest = (0, part), (part, height - part)
        return (
            (t, up, down, whole),
            (t, down, up, whole),
            (t, across, across, whole),
            (down, up, far, lo),
            (up, down, far, hi),
            (across, up, xo + lax.rem(y + NY - 1, NY), rest),
            (across, down, xo + lax.rem(y + 1, NY), rest),
            (far, across, xo + lax.rem(y + 2, NY), whole),
            (up, across, xo + lax.rem(y + 1, NY), first),
            (down, across, xo + lax.rem(y + NY - 1, NY), first),
        )

    def plane(p):
        step = (p + 1) // 2
        return zmod(d + jnp.where(lax.rem(p, 2) == 1, step, -step))

    def is_kv(p):
        return isinstance(p, int) and p >= NZ

    def xy(kind, p, incoming=False):
        buf = kvl.at[p - NZ] if is_kv(p) else wg.at[plane(jnp.int32(p))]
        block, to, arrives, (at, size) = kinds(buf.shape[0])[kind]
        view = buf.at[pl.ds(at, size), cols(arrives if incoming else block)]
        src = w_ref.at[:, cols(d)] if isinstance(p, int) and p == 0 and kind < 3 and not incoming else view
        return remote(src, view, xs.at[kind, p], xr.at[kind, p], tensor=to)

    def z_copy(p, which, incoming=False):
        step = (p + 1) // 2
        j = zmod(d + jnp.where(lax.rem(p, 2) == 1, -step, step))
        home = plane(p) if incoming else d
        if which == 0:
            src, dst = w_ref.at[:, cols(j)], wg.at[home, :, cols(t)]
        else:
            src, dst = kv_ref.at[which - 1, cols(j), :], kvl.at[which - 1, cols(home), cols(t)]
        return remote(src, dst, zs.at[which, p], zr.at[which, p], dp=j)

    def stage_a(p):
        if is_kv(p):
            for other in range(1, NZ):
                z_copy(jnp.int32(other), p - NZ + 1, True).wait_recv()
        else:
            z_copy(p, 0, True).wait_recv()
        for kind in (0, 1, 2):
            xy(kind, p).start()

    def stage_b(p):
        xy(0, p, True).wait_recv()
        xy(3, p).start()
        xy(9, p).start()
        xy(1, p, True).wait_recv()
        xy(4, p).start()
        xy(8, p).start()
        xy(2, p, True).wait_recv()
        xy(5, p).start()
        xy(6, p).start()

    def stage_c(p):
        xy(3, p, True).wait_recv()
        xy(4, p, True).wait_recv()
        xy(7, p).start()

    def stage_d(p):
        for kind in (5, 6, 7, 8, 9):
            xy(kind, p, True).wait_recv()

    for kind in (0, 1, 2):
        xy(kind, 0).start()
    for p in range(1, AHEAD + 1):
        z_copy(jnp.int32(p), 0).start()

    patches = pix.shape[1]
    natural = lax.broadcasted_iota(jnp.int32, (patches, patches), 0)
    turned = lax.broadcasted_iota(jnp.int32, (patches, patches), 1)
    per = patches // slot
    back = jnp.where(natural == lax.rem(turned, per) * slot + turned // per, 1.0, 0.0).astype(BF16)
    load_pixels.wait()
    pixels = dot_nt(back, pix[...].astype(BF16)).astype(BF16)
    load_patch.wait()
    embed = dot(pixels, patch_w[...])
    centered = embed - jnp.mean(embed, -1, keepdims=True)
    inv_dev = lax.rsqrt(jnp.mean(centered * centered, -1, keepdims=True) + 1e-06)
    normalized = centered * inv_dev
    xhat[...] = normalized
    visual = (normalized * vgain[...]).astype(BF16)
    for s in range(NZ):
        j, h = s // 2, s % 2
        tok[d, s] = visual[j * slot : (j + 1) * slot, h * rows : (h + 1) * rows]

    def ring_gather(buf, send, recv, views):
        n = len(views)

        def copy(src, k, side, c):
            view = buf.at[(src,) + views[c]]
            to = zmod(d + 1 - 2 * side)
            return remote(view, view, send.at[side, k - 1, c], recv.at[side, k - 1, c], dp=to)

        def order(k, side):
            own_half = list(range(side * n // 2, (side + 1) * n // 2))
            return own_half if k == NZ // 2 else own_half + [c for c in range(n) if c not in own_half]

        def go(k):
            for i in range(n):
                for side in (0, 1):
                    if i < len(order(k, side)):
                        start(copy(zmod(d - (1 - 2 * side) * (k - 1)), k, side, order(k, side)[i]))

        def arrive(k, then_go=False):
            for i in range(n):
                for side in (0, 1):
                    if i < len(order(k, side)):
                        src, c = zmod(d - (1 - 2 * side) * k), order(k, side)[i]
                        copy(src, k, side, c).wait_recv()
                        if then_go and c in order(k + 1, side):
                            start(copy(src, k + 1, side, c))

        return go, arrive

    go, arrive = ring_gather(tok, as_, ar, [(pl.ds(0, NZ // 2),), (pl.ds(NZ // 2, NZ // 2),)])
    go(1)
    heads = q_ref.shape[1] // L
    heads_in[0] = jnp.concatenate([q_ref[:, h * L : (h + 1) * L] for h in range(heads)], axis=0)
    masked = (cot_ref[...].astype(F32) * mask_ref[...].astype(F32)).astype(BF16)
    heads_in[1] = jnp.concatenate([masked[:, h * L : (h + 1) * L] for h in range(heads)], axis=0)
    hid[...] = jnp.zeros_like(hid)
    for c in own:
        c.wait()

    def piece(p, carry):
        s = plane(p)
        hid[...] += dot(tok[:, s].reshape(ntok, rows), wg[s])
        return carry

    def pieces(start_at, stop_at):
        lax.fori_loop(start_at, stop_at, piece, 0)

    def weights_step(i, carry):
        stage_a(i)

        @pl.when(i + AHEAD < NZ)
        def _():
            z_copy(i + AHEAD, 0).start()

        stage_b(i - 1)

        @pl.when(i >= 2)
        def _():
            stage_c(i - 2)

        @pl.when(i >= 3)
        def _():
            stage_d(i - 3)

        return carry

    at = 1
    for k, stop in enumerate(STOPS):
        lax.fori_loop(at, stop, weights_step, 0)
        arrive(k + 1, k < 3)
        if k in (1, 2):
            for p in range(1, NZ):
                start(z_copy(jnp.int32(p), k))
        at = stop
    stage_a(NZ)
    stage_b(NZ - 1)
    stage_c(NZ - 2)
    pieces(0, 3)
    stage_d(NZ - 3)
    stage_a(NZ + 1)
    stage_b(NZ)
    stage_c(NZ - 1)
    pieces(3, 6)
    stage_d(NZ - 2)
    stage_b(NZ + 1)
    stage_c(NZ)
    pieces(6, 7)
    stage_d(NZ - 1)
    pieces(7, NZ)
    stage_c(NZ + 1)

    hidden = hid[...].astype(BF16).astype(F32)
    hid[...] = hidden
    gain = jnp.concatenate(
        [gain_ref[:, pl.ds(pl.multiple_of((b * NZ + d) * L, L), L)] for b in range(NT)], axis=-1
    )
    total_sq = jnp.sum(hidden * hidden, -1, keepdims=True)
    ssq_s[...] = jnp.broadcast_to(total_sq, (ntok, L)).reshape(NZ, slot, L)
    for r in range(1, NZ):
        j = zmod(d + r)
        start(remote(ssq_s.at[j], ssq_r.at[d], sqs.at[r], sqr.at[r], dp=j))
    ssq_r[d] = ssq_s[d]
    scaled = (hidden * gain).astype(BF16)
    def ring_sum(part, sbuf, rbuf, send, recv, chunks, n):
        def copy(k, c, side):
            sign = 1 - 2 * side
            if k == 1:
                at = pl.ds((2 * c + side) * n, n)
            else:
                at = pl.ds(2 * c * n, 2 * n)
            return remote(
                sbuf.at[side, k - 1, at],
                rbuf.at[side, k - 1, at],
                send.at[side, k - 1, c],
                recv.at[side, k - 1, c],
                dp=zmod(d + sign),
            )

        def step(k, c):
            for side in (0, 1):
                sign = 1 - 2 * side
                e = zmod(d + sign * (NZ // 2 + 1 - k))
                if k > 1:
                    copy(k - 1, c, side).wait_recv()
                for b in range(2):
                    at = pl.ds((2 * c + b) * n, n)
                    if k == 1 and b != side:
                        continue
                    value = part[e, at]
                    if k > 2 or (k == 2 and b == side):
                        value = value + rbuf[side, k - 2, at].astype(F32)
                    sbuf[side, k - 1, at] = value.astype(BF16)
                start(copy(k, c, side))

        def result(c):
            at = pl.ds(2 * c * n, 2 * n)
            value = part[d, at]
            for side in (0, 1):
                copy(NZ // 2, c, side).wait_recv()
                value = value + rbuf[side, NZ // 2 - 1, at].astype(F32)
            return value

        return step, result

    chunks = NZ // 2
    step, result = ring_sum(part1, s1, r1, rs1s, rs1r, chunks, 1)
    for k in range(2):
        stage_d(NZ + k)
        mine = (2 * k, 2 * k + 1)
        for c in mine:
            at = c % 2 * 4 * L
            share = dot(scaled, kvl[k, :, at : at + 4 * L])
            for b in range(2):
                part1[:, 2 * c + b] = share[:, 2 * b * L : 2 * (b + 1) * L].reshape(NZ, slot, 2 * L)
            step(1, c)
    for i in range(2, NZ // 2 + 1):
        for c in range(chunks):
            step(i, c)
    for r in range(1, NZ):
        j = zmod(d - r)
        remote(ssq_s.at[j], ssq_r.at[j], sqs.at[r], sqr.at[r], dp=j).wait_recv()
    width = gain_ref.shape[1]
    root = lax.rsqrt(jnp.sum(ssq_r[...], axis=0) / width + 1e-06)[:, :1]
    for c in range(chunks):
        pre = result(c)
        for b in range(2):
            at = (c % 2 * 2 + b) * 2 * L
            kvpre[c // 2, :, at : at + 2 * L] = pre[b]
            kvt[c // 2, :, at : at + 2 * L] = (pre[b] * root).astype(BF16)

    for r in range(1, NT):
        j = lax.rem(t + r, NT)
        start(remote(kvt.at[:, :, cols(j)], kvh.at[t], ats.at[r], atr.at[r], tensor=j))
    kvh[t] = kvt[:, :, cols(t)]
    query, grad_out = heads_in[0], heads_in[1]
    for r in range(1, NT):
        j = lax.rem(t + NT - r, NT)
        remote(kvh.at[j], kvh.at[j], ats.at[r], atr.at[r], tensor=j).wait_recv()
    scale = 1.0 / math.sqrt(L)
    keys = kvh[:, 0].reshape(ntok, L)
    values = kvh[:, 1].reshape(ntok, L)
    scores = dot_nt(keys, query) * scale
    e = jnp.exp(scores - jnp.max(scores, axis=0, keepdims=True))
    probs = e / jnp.sum(e, axis=0, keepdims=True)
    grad_probs = dot_nt(values, grad_out)
    inner = jnp.sum(probs * grad_probs, axis=0, keepdims=True)
    grad_scores = (probs * (grad_probs - inner) * scale).astype(BF16)
    gkvh[:, 0] = dot(grad_scores, query).astype(BF16).reshape(NT, slot, L)
    gkvh[:, 1] = dot(probs.astype(BF16), grad_out).astype(BF16).reshape(NT, slot, L)
    for r in range(1, NT):
        j = lax.rem(t + r, NT)
        start(remote(gkvh.at[j], gkv.at[d, :, :, cols(t)], bts.at[r], btr.at[r], tensor=j))
    gkv[d, :, :, cols(t)] = gkvh[t]
    for r in range(1, NT):
        j = lax.rem(t + NT - r, NT)
        remote(gkvh.at[j], gkv.at[d, :, :, cols(j)], bts.at[r], btr.at[r], tensor=j).wait_recv()

    spans = [(k, slice(None), pl.ds(h * 4 * L, 4 * L)) for k in range(2) for h in range(2)]
    go, arrive = ring_gather(gkv, ags, agr, spans)
    go(1)
    products = gkv[d].astype(F32) * kvpre[...]
    row_sum = jnp.sum(products[0] + products[1], -1, keepdims=True)
    coef = root * root * root * row_sum / width
    lane = lax.broadcasted_iota(jnp.int32, (slot, L), 1)
    scal[d] = jnp.where(lane < L // 2, root, coef)
    for r in range(1, NZ):
        start(remote(scal.at[d], scal.at[d], scs.at[r], scr.at[r], dp=zmod(d + r)))
    for k in range(1, NZ // 2):
        arrive(k, True)
    arrive(NZ // 2)
    for r in range(1, NZ):
        j = zmod(d - r)
        remote(scal.at[j], scal.at[j], scs.at[r], scr.at[r], dp=j).wait_recv()
    grad_feat = dot_nt(gkv[:, 0].reshape(ntok, NT * L), kvl[0]) + dot_nt(
        gkv[:, 1].reshape(ntok, NT * L), kvl[1]
    )
    both = scal[...].reshape(ntok, L)
    grad_hidden = (both[:, :1] * gain * grad_feat - hid[...] * both[:, L - 1 :]).astype(BF16)

    step, result = ring_sum(part4, s4, r4, rs4s, rs4r, chunks, 1)
    for c in range(chunks):
        for b in range(2):
            s = 2 * c + b
            part4[:, s] = dot_nt(grad_hidden, wg[s]).reshape(NZ, slot, rows)
        step(1, c)
    for k in range(2, NZ // 2 + 1):
        for c in range(chunks):
            step(k, c)
    for c in range(chunks):
        value = result(c)
        gain_grad = jnp.concatenate([value[0], value[1]], axis=-1) * vgain[...]
        mine = pl.ds(c * slot, slot)
        normalized = xhat[mine, :]
        embed_grad = (
            inv_dev[c * slot : (c + 1) * slot]
            * (
                gain_grad
                - jnp.mean(gain_grad, -1, keepdims=True)
                - normalized * jnp.mean(gain_grad * normalized, -1, keepdims=True)
            )
        ).astype(BF16)
        gbuf[g, mine] = dot_nt(embed_grad, patch_w[...]).astype(BF16)
        for r in range(1, ng):
            view = gbuf.at[g, mine]
            start(remote(view, view, grs.at[r, c], grr.at[r, c], group=lax.rem(g + r, ng)))
    for c in range(chunks):
        for r in range(1, ng):
            j = lax.rem(g + ng - r, ng)
            view = gbuf.at[j, pl.ds(c * slot, slot)]
            remote(view, view, grs.at[r, c], grr.at[r, c], group=j).wait_recv()
    gradient = lax.dot_general(
        gbuf[...].reshape(ng * patches, -1),
        jnp.concatenate([back] * ng, axis=0),
        (((0,), (0,)), ((), ())),
        preferred_element_type=F32,
    )
    sqb[t] = jnp.broadcast_to(jnp.sum(gradient * gradient), (8, L))
    for r in range(1, NT):
        start(remote(sqb.at[t], sqb.at[t], fs.at[r], fr.at[r], tensor=lax.rem(t + r, NT)))
    for r in range(1, NT):
        j = lax.rem(t + NT - r, NT)
        remote(sqb.at[j], sqb.at[j], fs.at[r], fr.at[r], tensor=j).wait_recv()
    squares = jnp.sum(sqb[...], axis=0)[:1, :1]
    dir_ref[...] = gradient * lax.rsqrt(squares / n_pixels + 1e-06)
    store = pltpu.make_async_copy(dir_ref, dir_hbm.at[:, 0, :], local_sem.at[5])
    store.start()
    store.wait()

    for copy in sent:
        copy.wait_send()

    def drain(p, carry):
        for kind in range(10):
            xy(kind, p).wait_send()

        @pl.when(p > 0)
        def _():
            z_copy(p, 0).wait_send()

        return carry

    lax.fori_loop(0, NZ, drain, 0)
    for p in (NZ, NZ + 1):
        for kind in range(10):
            xy(kind, p).wait_send()


def body(
    images,
    step_size,
    member_mask,
    patch_weight,
    vision_norm_gain,
    merger_weight,
    norm_gain,
    kv_weight,
    queries,
    cotangent,
    *,
    ng,
):
    patches, pixels = images.shape[1:]
    slot = patches // 4
    rows, width = merger_weight.shape[1:]
    vwidth = patch_weight.shape[2]
    half = NZ // 2
    dma = pltpu.SemaphoreType.DMA
    vmem = pl.BlockSpec(memory_space=pltpu.VMEM)
    anywhere = pl.BlockSpec(memory_space=pl.ANY)
    normed = pl.pallas_call(
        functools.partial(kernel, ng, float(NT * patches * pixels)),
        out_shape=jax.ShapeDtypeStruct((pixels, 1, patches), F32),
        in_specs=[anywhere, anywhere, vmem, anywhere, vmem, anywhere, vmem, vmem, vmem],
        out_specs=anywhere,
        scratch_shapes=[
            pltpu.VMEM((NZ, rows, NT * L), BF16),
            pltpu.VMEM((2, NZ * L, NT * L), BF16),
            pltpu.VMEM((NZ, NZ, slot, rows), BF16),
            pltpu.VMEM((NZ * slot, NT * L), F32),
            pltpu.VMEM((NZ, NZ, slot, 2 * L), F32),
            pltpu.VMEM((2, half, NZ, slot, 2 * L), BF16),
            pltpu.VMEM((2, half, NZ, slot, 2 * L), BF16),
            pltpu.VMEM((NZ, slot, L), F32),
            pltpu.VMEM((NZ, slot, L), F32),
            pltpu.VMEM((2, slot, NT * L), F32),
            pltpu.VMEM((2, slot, NT * L), BF16),
            pltpu.VMEM((NT, 2, slot, L), BF16),
            pltpu.VMEM((NT, 2, slot, L), BF16),
            pltpu.VMEM((NZ, 2, slot, NT * L), BF16),
            pltpu.VMEM((NZ, slot, L), F32),
            pltpu.VMEM((NZ, NZ, slot, rows), F32),
            pltpu.VMEM((2, half, NZ, slot, rows), BF16),
            pltpu.VMEM((2, half, NZ, slot, rows), BF16),
            pltpu.VMEM((patches, vwidth), F32),
            pltpu.VMEM((ng, patches, pixels), BF16),
            pltpu.VMEM((NT, 8, L), F32),
            pltpu.VMEM((pixels, vwidth), BF16),
            pltpu.VMEM((2, NZ * slot, L), BF16),
            pltpu.VMEM((pixels, patches), F32),
            pltpu.VMEM((pixels, patches), F32),
            dma((6,)),
            dma((3, NZ)),
            dma((3, NZ)),
            dma((10, NZ + 2)),
            dma((10, NZ + 2)),
            dma((2, half, 2)),
            dma((2, half, 2)),
            dma((2, half, half)),
            dma((2, half, half)),
            dma((NZ,)),
            dma((NZ,)),
            dma((NT,)),
            dma((NT,)),
            dma((NT,)),
            dma((NT,)),
            dma((2, half, half)),
            dma((2, half, half)),
            dma((NZ,)),
            dma((NZ,)),
            dma((2, half, half)),
            dma((2, half, half)),
            dma((max(ng, 2), half)),
            dma((max(ng, 2), half)),
            dma((NT,)),
            dma((NT,)),
        ],
        compiler_params=pltpu.CompilerParams(
            collective_id=0, has_side_effects=True, vmem_limit_bytes=60 * 1024 * 1024
        ),
    )(
        images.transpose(2, 0, 1),
        patch_weight[0],
        vision_norm_gain,
        merger_weight[0],
        norm_gain,
        kv_weight[0],
        queries[0, 0],
        cotangent[0, 0],
        member_mask,
    )
    direction = jnp.tanh(normed.transpose(1, 2, 0))
    adversarial = jnp.clip(images + step_size[:, None, None] * direction, 0.0, 1.0)
    return adversarial, direction


def solution(mesh):
    placed = (
        P("dp", "tensor", None),
        P("dp"),
        P("group", "dp"),
        P("group", None, None),
        P("group", None),
        P("group", "dp", "tensor"),
        P("group", None),
        P("group", None, "dp", "tensor"),
        P("group", "dp", None, "tensor"),
        P("group", "dp", None, "tensor"),
    )
    return jax.shard_map(
        functools.partial(body, ng=mesh.shape["group"]),
        mesh=mesh,
        in_specs=placed,
        out_specs=(P("dp", "tensor", None), P("dp", "tensor", None)),
        check_vma=False,
    )
```
